32 devices in a mesh: grp: 2 (over y), sub: 16 (over z, x, core).
Axes of the slice: x: 2, y: 2, z: 4, core: 2. Of those that a mesh axis runs over, the one named last changes fastest.
Arguments:
- right_sides: float32 [16384, 128], P(('grp', 'sub')), may hold values from -6 to 6
- basis_u: bfloat16 [5, 16384, 256], P(None, ('grp', 'sub')), may hold values from -0.15625 to 0.15625
- basis_v: bfloat16 [5, 16384, 256], P(None, ('grp', 'sub')), may hold values from -0.25 to 0.25
- coupling: bfloat16 [5, 8192, 512], P(None, ('grp', 'sub')), may hold values from -0.13258252 to 0.13258252, as said below
Outputs:
- solution: float32 [16384, 128], P(('grp', 'sub'))
The draws below stay inside these ranges and needn't reach their ends.
Inputs may be any that keep to these rules, and one draw needn't show every extreme that they name: For level l the 256 rows of coupling on a device equal those on every device whose index (grp major) agrees with it in all bits from bit 5 - 5 + l upwards. Entries of level l are independent, of mean 0 and deviation (2 * 256 * 2**(0 + l))**-0.5, and lie within three such deviations.
All inputs are finite; a program needn't handle non-finite values.
Results may differ from the reference program's by a relative error of at most 0.0003.
Values sent between devices are 32-bit elements; how exact they have to be, the bound alone decides.
No kernel may reach another device: no remote copies, remote signals or barrier semaphores. Data moves between devices by JAX's collectives and lax.ppermute only.
A program may use at most 64 MiB of HBM per device.

```python
import jax
import jax.numpy as jnp
from jax import lax

RANK = 256
PTS_DEV = 512
COLS = 128
LEVELS = 5
BITS = 5
ROWS = 16384
N_GRP = 2
N_SUB = 16


def draw_coupling(key, part):
    key = jax.random.fold_in(key, 11)
    devices = N_GRP * N_SUB
    blocks = []
    for height in range(LEVELS):
        span_bits = BITS - LEVELS + height
        group_ids = jnp.arange(devices) // 2 ** span_bits
        level_key = jax.random.fold_in(key, height)
        keys = jax.vmap(lambda group: jax.random.fold_in(level_key, group))(group_ids)
        scale = (2.0 * RANK * 2 ** span_bits) ** (-0.5)
        values = jax.vmap(lambda one: jnp.clip(jax.random.normal(one, (RANK, 2 * RANK), jnp.float32), -2.99, 2.99))(keys)
        blocks.append((values * scale).reshape(devices * RANK, 2 * RANK).astype(jnp.bfloat16))
    return jnp.stack(blocks)


def block_levels(own_key, shape, cuts, low, top_value):
    def one(dim, blocks):
        draws = jax.random.uniform(jax.random.fold_in(jax.random.fold_in(own_key, 6), dim), (blocks,), jnp.float32, low / len(cuts), top_value / len(cuts))
        return jnp.repeat(jnp.exp(draws), shape[dim] // blocks).reshape((-1,) + (1,) * (len(shape) - dim - 1))

    level = one(*cuts[0])
    for cut in cuts[1:]:
        level = level * one(*cut)
    return level


def scatter_about(own_key, extent, deviation, bound, shards=(), kind=jnp.bfloat16):
    level = block_levels(own_key, extent, shards, -0.22, 0.18) if shards else 1.0
    array = jax.random.normal(own_key, extent, jnp.float32) * deviation * level
    return jnp.minimum(jnp.maximum(array, -bound), bound).astype(kind)


def setup_inputs(seed: int = 0) -> dict:
    arg_keys = jax.random.split(jax.random.key(seed), 5)
    right_sides = scatter_about(arg_keys[0], (ROWS, COLS), 1.0, 6.0, ((0, 32),), jnp.float32)
    basis_u = scatter_about(arg_keys[1], (LEVELS, ROWS, RANK), (RANK * LEVELS) ** -0.5, 0.15625, ((1, 32),))
    basis_v = scatter_about(arg_keys[2], (LEVELS, ROWS, RANK), PTS_DEV ** -0.5, 0.25, ((1, 32),))
    coupling = draw_coupling(jax.random.fold_in(arg_keys[4], 71), 0)
    return {"right_sides": right_sides, "basis_u": basis_u, "basis_v": basis_v, "coupling": coupling}


def reference(right_sides, basis_u, basis_v, coupling):
    devices = N_GRP * N_SUB
    highest = lax.Precision.HIGHEST
    current = right_sides.reshape(devices, PTS_DEV, COLS)
    for height in range(LEVELS):
        span_bits = BITS - LEVELS + height
        v_basis = basis_v[height].astype(jnp.float32).reshape(devices, PTS_DEV, RANK)
        u_basis = basis_u[height].astype(jnp.float32).reshape(devices, PTS_DEV, RANK)
        couple_rows = coupling[height].astype(jnp.float32).reshape(devices, RANK, 2 * RANK)
        partial_value = jnp.einsum("dpr,dpn->drn", v_basis, current, precision=highest)
        group_sums = partial_value.reshape(devices // (2 ** span_bits), 2 ** span_bits, RANK, COLS).sum(axis=1)
        node_sums = group_sums.reshape(devices // (2 ** (span_bits + 1)), 2 * RANK, COLS)
        spread = jnp.repeat(node_sums, 2 ** (span_bits + 1), axis=0)
        weights = jnp.einsum("drs,dsn->drn", couple_rows, spread, precision=highest)
        current = current - jnp.einsum("dpr,drn->dpn", u_basis, weights, precision=highest)
    return current.reshape(devices * PTS_DEV, COLS)
```

```python
import functools

import jax
import jax.numpy as jnp
from jax import lax
from jax.experimental import pallas as pl
from jax.experimental.pallas import tpu as pltpu
from jax.sharding import PartitionSpec as P

F32 = jnp.float32
BF16 = jnp.bfloat16
AXES = ("grp", "sub")


def swapped(value, axis, bit):
    mask = 2**bit
    pairs = [(source, source ^ mask) for source in range(lax.axis_size(axis))]
    return lax.ppermute(value, axis, pairs)


def partner(value, bit, sub_bits):
    if bit < sub_bits:
        return swapped(value, "sub", bit)
    return swapped(value, "grp", bit - sub_bits)


def pairwise(own_sum, first_bit, span_bits, sub_bits, lower_half):
    for bit in range(first_bit, span_bits):
        own_sum = own_sum + partner(own_sum, bit, sub_bits)
    other_sum = partner(own_sum, span_bits, sub_bits)
    first_half = jnp.where(lower_half, own_sum, other_sum)
    second_half = jnp.where(lower_half, other_sum, own_sum)
    return jnp.concatenate([first_half, second_half], axis=0)


def bit_by_bit(right_sides, basis_u, basis_v, coupling):
    highest = lax.Precision.HIGHEST
    sub_bits = lax.axis_size("sub").bit_length() - 1
    all_bits = sub_bits + lax.axis_size("grp").bit_length() - 1
    levels = basis_u.shape[0]
    position = lax.axis_index("grp") * lax.axis_size("sub") + lax.axis_index("sub")
    current = right_sides
    for height in range(levels):
        span_bits = all_bits - levels + height
        v_basis = basis_v[height].astype(F32)
        own_sum = jnp.einsum("pr,pn->rn", v_basis, current, precision=highest)
        lower_half = jnp.bitwise_and(jnp.right_shift(position, span_bits), 1) == 0
        node_sum = pairwise(own_sum, 0, span_bits, sub_bits, lower_half)
        weights = jnp.dot(coupling[height].astype(F32), node_sum, precision=highest)
        current = current - jnp.dot(basis_u[height].astype(F32), weights, precision=highest)
    return current


def split(value):
    high = value.astype(BF16)
    low = (value - high.astype(F32)).astype(BF16)
    return high, low


def stacked(value):
    return jnp.concatenate(split(value), axis=0)


def folded(value):
    half = value.shape[0] // 2
    return value[:half] + value[half:]


def dot(left, right):
    return lax.dot_general(left, right, (((1,), (0,)), ((), ())), preferred_element_type=F32)


def dot_transposed(left, right):
    return lax.dot_general(left, right, (((1,), (1,)), ((), ())), preferred_element_type=F32)


def weights_of(lower, upper, couple):
    rank = couple.shape[0]
    lower, upper = stacked(lower), stacked(upper)
    return folded(dot_transposed(lower, couple[:, :rank]) + dot_transposed(upper, couple[:, rank:]))


def correction(weights, cross):
    high, low = split(cross)
    both = stacked(weights)
    return folded(dot(both, high) + dot(both, low))


def bit_is_set(axis, bit):
    return jnp.bitwise_and(jnp.right_shift(lax.axis_index(axis), bit), 1) == 1


def ordered(flag, own, other):
    return jnp.where(flag, other, own), jnp.where(flag, own, other)


def start_kernel(right_hbm, u_hbm, v_hbm, c_hbm, current_ref, sum_ref, u_ref, v_ref, c_ref, right_ref,
                 first_ref, sems):
    sources = [right_hbm, v_hbm.at[0], v_hbm.at[1], u_hbm.at[0], c_hbm.at[0]]
    targets = [right_ref, first_ref, v_ref, u_ref, c_ref]
    copies = [pltpu.make_async_copy(*pair, sems.at[place]) for place, pair in enumerate(zip(sources, targets))]
    for copy in copies:
        copy.start()
    copies[0].wait()
    current = right_ref[...].T
    current_ref[...] = current
    copies[1].wait()
    sum_ref[...] = folded(dot(stacked(current), first_ref[...]))
    for copy in copies[2:]:
        copy.wait()


def first_sum_kernel(current_ref, u_ref, v_ref, sum_ref, cross_ref):
    sum_ref[...] = folded(dot(stacked(current_ref[...]), v_ref[...]))
    cross_ref[...] = dot(u_ref[...].T, v_ref[...])


def pair_kernel(own_ref, other_ref, c_ref, sum_ref, cross_ref, weights_ref, keep_ref, send_ref):
    upper_core = bit_is_set("sub", 0)
    half = keep_ref.shape[0]
    weights = weights_of(*ordered(upper_core, own_ref[...], other_ref[...]), c_ref[...])
    weights_ref[...] = weights
    later = sum_ref[...] - correction(weights, cross_ref[...])
    keep_ref[...], send_ref[...] = ordered(upper_core, later[:half], later[half:])


def later_sums_kernel(current_ref, weights_ref, u_ref, v_ref, keep_ref, send_ref):
    upper_core = bit_is_set("sub", 0)
    half = keep_ref.shape[1]
    current = current_ref[...] - folded(dot_transposed(stacked(weights_ref[...]), u_ref[0]))
    current = stacked(current)
    for place in range(keep_ref.shape[0]):
        later = folded(dot(current, v_ref[place + 2]))
        keep_ref[place], send_ref[place] = ordered(upper_core, later[:half], later[half:])


def cross_kernel(u_ref, v_ref, early_ref, late_ref, keep_ref, send_ref):
    upper_core = bit_is_set("sub", 0)
    first, second, third = u_ref[1].T, u_ref[2].T, u_ref[3].T
    early_ref[0] = dot(first, v_ref[2])
    early_ref[1] = dot(first, v_ref[3])
    late_ref[0] = dot(first, v_ref[4])
    late_ref[1] = dot(second, v_ref[4])
    keep_ref[...], send_ref[...] = ordered(upper_core, dot(second, v_ref[3]), dot(third, v_ref[4]))


def first_weights_kernel(own_ref, across_ref, c_ref, weights_ref):
    lower, upper = ordered(bit_is_set("sub", 1), own_ref[...], across_ref[...])
    weights_ref[...] = weights_of(lower, upper, c_ref[1])


def square_weights_kernel(level, axis, bit, own_count, *refs):
    *part_refs, c_ref, weights_ref = refs
    parts = [ref[0] if len(ref.shape) == 3 else ref[...] for ref in part_refs]
    own, other = sum(parts[1:own_count], parts[0]), sum(parts[own_count + 1 :], parts[own_count])
    weights_ref[...] = weights_of(*ordered(bit_is_set(axis, bit), own, other), c_ref[level])


def in_turn(first, second):
    return ordered(bit_is_set("sub", 0), first, second)


def second_weights_kernel(own_ref, first_ref, second_ref, both_ref, c_ref, weights_ref):
    beside, across = in_turn(first_ref[0], second_ref[0])
    own, other = own_ref[...] + beside, across + both_ref[...]
    weights_ref[...] = weights_of(*ordered(bit_is_set("sub", 2), own, other), c_ref[2])


def second_third_kernel(weights_ref, early_ref, got_ref, sums_ref, got_sums_ref, second_ref, pair_ref):
    weights = weights_ref[...]
    second_ref[...] = sums_ref[0] + got_sums_ref[0] - correction(weights, early_ref[0] + got_ref[0])
    pair_ref[0] = second_ref[...]
    pair_ref[1] = sums_ref[1] + got_sums_ref[1] - correction(weights, early_ref[1] + got_ref[1])


def fourth_kernel(weights_ref, late_ref, got_ref, sums_ref, got_sums_ref, fourth_ref, cross_ref):
    fourth_ref[...] = sums_ref[2] + got_sums_ref[2] - correction(weights_ref[...], late_ref[0] + got_ref[0])
    cross_ref[...] = late_ref[1] + got_ref[1]


def third_fourth_kernel(weights_ref, mixed_ref, mixed_got_ref, pair_ref, first_ref, second_ref, fourth_ref, cross_ref,
                        third_ref, later_ref):
    weights = weights_ref[...]
    cross, _ = ordered(bit_is_set("sub", 0), mixed_ref[...], mixed_got_ref[...])
    beside, _ = in_turn(first_ref[1], second_ref[1])
    third_ref[...] = pair_ref[1] + beside - correction(weights, cross)
    later_ref[...] = fourth_ref[...] - correction(weights, cross_ref[...])


def last_sum_kernel(weights_ref, sum_ref, cross_ref, cross_got_ref, later_ref):
    _, cross = ordered(bit_is_set("sub", 0), cross_ref[...], cross_got_ref[...])
    later_ref[...] = sum_ref[...] - correction(weights_ref[...], cross)


def stack_kernel(first_ref, second_ref, third_ref, out_ref):
    out_ref[0], out_ref[1], out_ref[2] = first_ref[...], second_ref[...], third_ref[...]


def columns_of(own, other):
    lower, upper = ordered(bit_is_set("sub", 0), own, other)
    return jnp.concatenate(split(jnp.concatenate([lower, upper], axis=0).T), axis=1)


def fold_columns(value):
    half = value.shape[1] // 2
    return value[:, :half] + value[:, half:]


def gather_kernel(right_ref, u_ref, first_ref, own_ref, other_ref, out_ref):
    total = dot(u_ref[0], jnp.concatenate(split(first_ref[...].T), axis=1))
    for place in range(own_ref.shape[0]):
        total = total + dot(u_ref[place + 1], columns_of(own_ref[place], other_ref[place]))
    out_ref[...] = right_ref[...] - fold_columns(total)


def last_kernel(level, chunks, partial_ref, own_ref, other_ref, u_ref, out_hbm, out_ref, sems):
    weights = columns_of(own_ref[...], other_ref[...])
    rows = out_ref.shape[0] // chunks
    copies = []
    for place in range(chunks):
        part = pl.ds(place * rows, rows)
        out_ref[part] = partial_ref[part] - fold_columns(dot(u_ref[level, part], weights))
        copies.append(pltpu.make_async_copy(out_ref.at[part], out_hbm.at[part], sems.at[place]))
        copies[-1].start()
    for copy in copies:
        copy.wait()


def run_last(level, partial, own, other, basis_u):
    vmem, chunks = pl.BlockSpec(memory_space=pltpu.VMEM), 4
    return pl.pallas_call(
        functools.partial(last_kernel, level, chunks),
        out_shape=jax.ShapeDtypeStruct(partial.shape, F32),
        in_specs=[vmem] * 4,
        out_specs=pl.BlockSpec(memory_space=pl.ANY),
        scratch_shapes=[pltpu.VMEM(partial.shape, F32), pltpu.SemaphoreType.DMA((chunks,))],
        compiler_params=pltpu.CompilerParams(vmem_limit_bytes=2 * 2**20),
    )(partial, own, other, basis_u)


def run(kernel, outs, *args, after=(), flops=0):
    vmem, unread = pl.BlockSpec(memory_space=pltpu.VMEM), pl.BlockSpec(memory_space=pl.ANY)
    return pl.pallas_call(
        lambda *refs: kernel(*refs[: len(args)], *refs[len(args) + len(after) :]),
        out_shape=[jax.ShapeDtypeStruct(shape, F32) for shape in outs],
        in_specs=[vmem] * len(args) + [unread] * len(after),
        out_specs=[vmem] * len(outs),
        cost_estimate=pl.CostEstimate(flops=flops, bytes_accessed=0, transcendentals=0) if flops else None,
        compiler_params=pltpu.CompilerParams(vmem_limit_bytes=2 * 2**20),
    )(*args, *after)


def add_kernel(first_ref, second_ref, out_ref):
    out_ref[...] = first_ref[...] + second_ref[...]


def first_of_kernel(first_ref, second_ref, out_ref):
    out_ref[...] = first_ref[...] + second_ref[0]


def added(first, second, **options):
    return run(add_kernel, [first.shape], first, second, **options)[0]


def run_start(right_sides, basis_u, basis_v, coupling):
    columns, (points, rank) = right_sides.shape[1], basis_u.shape[1:]
    shape = jax.ShapeDtypeStruct
    arrays = [pltpu.with_memory_space_constraint(value, pltpu.HBM)
              for value in (right_sides, basis_u, basis_v, coupling)]
    outs = [shape((columns, points), F32), shape((columns, rank), F32), shape((points, rank), BF16),
            shape((points, rank), BF16), shape(coupling.shape[1:], BF16), shape((points, columns), F32)]
    return pl.pallas_call(
        start_kernel,
        out_shape=outs,
        in_specs=[pl.BlockSpec(memory_space=pl.ANY)] * len(arrays),
        out_specs=[pl.BlockSpec(memory_space=pltpu.VMEM)] * len(outs),
        scratch_shapes=[pltpu.VMEM((points, rank), BF16), pltpu.SemaphoreType.DMA((5,))],
        compiler_params=pltpu.CompilerParams(vmem_limit_bytes=4 * 2**20),
    )(*arrays)


def tied(value, *others):
    return lax.optimization_barrier((value,) + others)[0]


def traded(value, mask):
    if mask < lax.axis_size("sub"):
        return lax.ppermute(value, "sub", [(source, source ^ mask) for source in range(lax.axis_size("sub"))])
    devices = lax.axis_size("grp") * lax.axis_size("sub")
    return lax.ppermute(value, AXES, [(source, source ^ mask) for source in range(devices)])


def crossed(value, even, odd):
    pairs = [(source, source ^ (odd if source & 1 else even)) for source in range(lax.axis_size("sub"))]
    return lax.ppermute(value, "sub", pairs)


def tree(right_sides, basis_u, basis_v, coupling):
    points, rank = basis_u.shape[1:]
    columns = right_sides.shape[1]
    half = columns // 2
    square, block = (rank, rank), (half, rank)

    current, own, u_first, v_second, couple, right_near = run_start(right_sides, basis_u, basis_v, coupling)
    other = traded(own, 1)
    first_sum, first_cross = run(first_sum_kernel, [(columns, rank), square], current, u_first, v_second)
    weights0, keep, send = run(
        pair_kernel, [(columns, rank), block, block], own, other, couple, first_sum, first_cross
    )
    got = traded(send, 1)
    early, late, keep_cross, send_cross = run(
        cross_kernel, [(2,) + square, (2,) + square, square, square], basis_u, basis_v, after=[weights0], flops=2 * 10**9
    )
    sums, sums_send = run(
        later_sums_kernel, [(3,) + block, (3,) + block], current, weights0, basis_u, basis_v,
        after=[keep_cross], flops=2 * 10**9,
    )
    sum1 = added(keep, got, after=[sums])

    across = traded(sum1, 2)
    cross_got = traded(tied(send_cross, sum1), 1)
    early_got = traded(tied(early, sum1), 1)
    sums_got = traded(tied(sums_send, sum1), 1)
    late_got = traded(tied(late, sum1), 1)
    mixed = added(keep_cross, cross_got, flops=2 * 10**9)
    mixed_across = crossed(mixed, 2, 4)
    (weights1,) = run(first_weights_kernel, [block], sum1, across, coupling, flops=8 * 10**9)
    second, pair = run(
        second_third_kernel, [block, (2,) + block], weights1, early, early_got, sums, sums_got
    )

    both, first_turn, second_turn = traded(second, 6), crossed(pair, 2, 4), crossed(pair, 4, 2)
    fourth, cross42 = run(
        fourth_kernel, [block, square], weights1, late, late_got, sums, sums_got, flops=2 * 10**9
    )
    mixed = added(mixed, mixed_across, after=[fourth])
    mixed_got = traded(mixed, 1)
    (weights2,) = run(
        second_weights_kernel, [block], second, first_turn, second_turn, both, coupling, flops=8 * 10**9
    )
    odd = [(source, source ^ 2) for source in range(1, lax.axis_size("sub"), 2)]
    cross43_got = lax.ppermute(mixed, "sub", odd)
    third, later4 = run(
        third_fourth_kernel, [block, block],
        weights2, mixed, mixed_got, pair, first_turn, second_turn, fourth, cross42,
    )

    sum4 = added(later4, traded(later4, 2), after=[third])
    sum4_got = traded(sum4, 4)
    both, across, beside = traded(third, 12), traded(third, 8), traded(third, 4)
    cross43 = added(mixed, cross43_got, after=[third])
    cross43_got = traded(cross43, 1)
    (weights3,) = run(
        functools.partial(square_weights_kernel, 3, "sub", 3, 2), [block], third, beside, across, both, coupling
    )
    sum4 = added(sum4, sum4_got, after=[weights3], flops=8 * 10**9)
    (sum4,) = run(last_sum_kernel, [block], weights3, sum4, cross43, cross43_got)

    both, beside, across = traded(sum4, 24), traded(sum4, 8), traded(sum4, 16)
    (three,) = run(stack_kernel, [(3,) + block], weights1, weights2, weights3, after=[sum4])
    three_got = traded(three, 1)
    (partial,) = run(
        gather_kernel, [(points, columns)], right_near, basis_u, weights0, three, three_got, flops=2 * 10**9
    )
    own_sum = added(sum4, beside, after=[both], flops=4 * 10**9)
    (weights4,) = run(
        functools.partial(square_weights_kernel, 4, "grp", 0, 1), [block], own_sum, across, both, coupling
    )
    return run_last(4, partial, weights4, traded(weights4, 1), basis_u)


def solution(mesh):
    n_grp, n_sub = mesh.shape["grp"], mesh.shape["sub"]

    def per_device(right_sides, basis_u, basis_v, coupling):
        if basis_u.shape[0] == 5 and n_grp == 2 and n_sub == 16:
            return tree(right_sides, basis_u, basis_v, coupling)
        return bit_by_bit(right_sides, basis_u, basis_v, coupling)

    in_specs = (P(AXES, None), P(None, AXES, None), P(None, AXES, None), P(None, AXES, None))
    return jax.shard_map(
        per_device, mesh=mesh, in_specs=in_specs, out_specs=P(AXES, None), check_vma=False
    )
```

```python
import functools

import jax
import jax.numpy as jnp
from jax import lax
from jax.experimental import pallas as pl
from jax.experimental.pallas import tpu as pltpu
from jax.sharding import PartitionSpec as P

F32 = jnp.float32
BF16 = jnp.bfloat16
AXES = ("grp", "sub")


def swapped(value, axis, bit):
    mask = 2**bit
    pairs = [(source, source ^ mask) for source in range(lax.axis_size(axis))]
    return lax.ppermute(value, axis, pairs)


def partner(value, bit, sub_bits):
    if bit < sub_bits:
        return swapped(value, "sub", bit)
    return swapped(value, "grp", bit - sub_bits)


def pairwise(own_sum, first_bit, span_bits, sub_bits, lower_half):
    for bit in range(first_bit, span_bits):
        own_sum = own_sum + partner(own_sum, bit, sub_bits)
    other_sum = partner(own_sum, span_bits, sub_bits)
    first_half = jnp.where(lower_half, own_sum, other_sum)
    second_half = jnp.where(lower_half, other_sum, own_sum)
    return jnp.concatenate([first_half, second_half], axis=0)


def bit_by_bit(right_sides, basis_u, basis_v, coupling):
    highest = lax.Precision.HIGHEST
    sub_bits = lax.axis_size("sub").bit_length() - 1
    all_bits = sub_bits + lax.axis_size("grp").bit_length() - 1
    levels = basis_u.shape[0]
    position = lax.axis_index("grp") * lax.axis_size("sub") + lax.axis_index("sub")
    current = right_sides
    for height in range(levels):
        span_bits = all_bits - levels + height
        v_basis = basis_v[height].astype(F32)
        own_sum = jnp.einsum("pr,pn->rn", v_basis, current, precision=highest)
        lower_half = jnp.bitwise_and(jnp.right_shift(position, span_bits), 1) == 0
        node_sum = pairwise(own_sum, 0, span_bits, sub_bits, lower_half)
        weights = jnp.dot(coupling[height].astype(F32), node_sum, precision=highest)
        current = current - jnp.dot(basis_u[height].astype(F32), weights, precision=highest)
    return current


def split(value):
    high = value.astype(BF16)
    low = (value - high.astype(F32)).astype(BF16)
    return high, low


def stacked(value):
    return jnp.concatenate(split(value), axis=0)


def folded(value):
    half = value.shape[0] // 2
    return value[:half] + value[half:]


def dot(left, right):
    return lax.dot_general(left, right, (((1,), (0,)), ((), ())), preferred_element_type=F32)


def dot_transposed(left, right):
    return lax.dot_general(left, right, (((1,), (1,)), ((), ())), preferred_element_type=F32)


def weights_of(lower, upper, couple):
    rank = couple.shape[0]
    lower, upper = stacked(lower), stacked(upper)
    return folded(dot_transposed(lower, couple[:, :rank]) + dot_transposed(upper, couple[:, rank:]))


def correction(weights, cross):
    high, low = split(cross)
    both = stacked(weights)
    return folded(dot(both, high) + dot(both, low))


def bit_is_set(axis, bit):
    return jnp.bitwise_and(jnp.right_shift(lax.axis_index(axis), bit), 1) == 1


def ordered(flag, own, other):
    return jnp.where(flag, other, own), jnp.where(flag, own, other)


def start_kernel(right_hbm, u_hbm, v_hbm, c_hbm, current_ref, sum_ref, u_ref, v_ref, c_ref, right_ref,
                 first_ref, sems):
    sources = [right_hbm, v_hbm.at[0], v_hbm.at[1], u_hbm.at[0], c_hbm.at[0]]
    targets = [right_ref, first_ref, v_ref, u_ref, c_ref]
    copies = [pltpu.make_async_copy(*pair, sems.at[place]) for place, pair in enumerate(zip(sources, targets))]
    for copy in copies:
        copy.start()
    copies[0].wait()
    current = right_ref[...].T
    current_ref[...] = current
    copies[1].wait()
    sum_ref[...] = folded(dot(stacked(current), first_ref[...]))
    for copy in copies[2:]:
        copy.wait()


def first_sum_kernel(current_ref, u_ref, v_ref, sum_ref, cross_ref):
    sum_ref[...] = folded(dot(stacked(current_ref[...]), v_ref[...]))
    cross_ref[...] = dot(u_ref[...].T, v_ref[...])


def pair_kernel(own_ref, other_ref, c_ref, sum_ref, cross_ref, weights_ref, keep_ref, send_ref):
    upper_core = bit_is_set("sub", 0)
    half = keep_ref.shape[0]
    weights = weights_of(*ordered(upper_core, own_ref[...], other_ref[...]), c_ref[...])
    weights_ref[...] = weights
    later = sum_ref[...] - correction(weights, cross_ref[...])
    keep_ref[...], send_ref[...] = ordered(upper_core, later[:half], later[half:])


def later_sums_kernel(current_ref, weights_ref, u_ref, v_ref, keep_ref, send_ref):
    upper_core = bit_is_set("sub", 0)
    half = keep_ref.shape[1]
    current = current_ref[...] - folded(dot_transposed(stacked(weights_ref[...]), u_ref[0]))
    current = stacked(current)
    for place in range(keep_ref.shape[0]):
        later = folded(dot(current, v_ref[place + 2]))
        keep_ref[place], send_ref[place] = ordered(upper_core, later[:half], later[half:])


def cross_kernel(u_ref, v_ref, early_ref, keep_ref, send_ref):
    upper_core = bit_is_set("sub", 0)
    first, second, third = u_ref[1].T, u_ref[2].T, u_ref[3].T
    early_ref[0] = dot(first, v_ref[2])
    early_ref[1] = dot(first, v_ref[3])
    early_ref[2] = dot(first, v_ref[4])
    early_ref[3] = dot(second, v_ref[4])
    rows = keep_ref.shape[1]
    for place, cross in enumerate((dot(second, v_ref[3]), dot(third, v_ref[4]))):
        keep_ref[place], send_ref[place] = ordered(upper_core, cross[:rows], cross[rows:])


def mix_kernel(keep_ref, got_ref, third_ref, fourth_ref):
    third_ref[...], fourth_ref[...] = keep_ref[0] + got_ref[0], keep_ref[1] + got_ref[1]


def both_added_kernel(third_ref, third_got_ref, fourth_ref, fourth_got_ref, third_out_ref, fourth_out_ref):
    third_out_ref[...] = third_ref[...] + third_got_ref[...]
    fourth_out_ref[...] = fourth_ref[...] + fourth_got_ref[...]


def whole(half_ref, got_ref):
    return jnp.concatenate(ordered(bit_is_set("sub", 0), half_ref[...], got_ref[...]), axis=0)


def first_weights_kernel(own_ref, across_ref, c_ref, weights_ref):
    lower, upper = ordered(bit_is_set("sub", 1), own_ref[...], across_ref[...])
    weights_ref[...] = weights_of(lower, upper, c_ref[1])


def square_weights_kernel(level, axis, bit, own_count, *refs):
    *part_refs, c_ref, weights_ref = refs
    parts = [ref[0] if len(ref.shape) == 3 else ref[...] for ref in part_refs]
    own, other = sum(parts[1:own_count], parts[0]), sum(parts[own_count + 1 :], parts[own_count])
    weights_ref[...] = weights_of(*ordered(bit_is_set(axis, bit), own, other), c_ref[level])


def second_third_kernel(weights_ref, early_ref, got_ref, sums_ref, got_sums_ref, second_ref, pair_ref):
    weights = weights_ref[...]
    second_ref[...] = sums_ref[0] + got_sums_ref[0] - correction(weights, early_ref[0] + got_ref[0])
    pair_ref[0] = second_ref[...]
    pair_ref[1] = sums_ref[1] + got_sums_ref[1] - correction(weights, early_ref[1] + got_ref[1])


def fourth_kernel(weights_ref, early_ref, got_ref, sums_ref, got_sums_ref, fourth_ref, cross_ref):
    fourth_ref[...] = sums_ref[2] + got_sums_ref[2] - correction(weights_ref[...], early_ref[2] + got_ref[2])
    cross_ref[...] = early_ref[3] + got_ref[3]


def third_fourth_kernel(weights_ref, half_ref, half_got_ref, pair_ref, beside_ref, fourth_ref, cross_ref,
                        third_ref, later_ref):
    weights = weights_ref[...]
    cross = whole(half_ref, half_got_ref)
    third_ref[...] = pair_ref[1] + beside_ref[1] - correction(weights, cross)
    later_ref[...] = fourth_ref[...] - correction(weights, cross_ref[...])


def last_sum_kernel(weights_ref, sum_ref, half_ref, half_got_ref, later_ref):
    later_ref[...] = sum_ref[...] - correction(weights_ref[...], whole(half_ref, half_got_ref))


def stack_kernel(first_ref, second_ref, third_ref, out_ref):
    out_ref[0], out_ref[1], out_ref[2] = first_ref[...], second_ref[...], third_ref[...]


def columns_of(own, other):
    lower, upper = ordered(bit_is_set("sub", 0), own, other)
    return jnp.concatenate(split(jnp.concatenate([lower, upper], axis=0).T), axis=1)


def fold_columns(value):
    half = value.shape[1] // 2
    return value[:, :half] + value[:, half:]


def gather_kernel(right_ref, u_ref, first_ref, own_ref, other_ref, out_ref):
    total = dot(u_ref[0], jnp.concatenate(split(first_ref[...].T), axis=1))
    for place in range(own_ref.shape[0]):
        total = total + dot(u_ref[place + 1], columns_of(own_ref[place], other_ref[place]))
    out_ref[...] = right_ref[...] - fold_columns(total)


def last_kernel(level, chunks, partial_ref, own_ref, other_ref, u_ref, out_hbm, out_ref, sems):
    weights = columns_of(own_ref[...], other_ref[...])
    rows = out_ref.shape[0] // chunks
    copies = []
    for place in range(chunks):
        part = pl.ds(place * rows, rows)
        out_ref[part] = partial_ref[part] - fold_columns(dot(u_ref[level, part], weights))
        copies.append(pltpu.make_async_copy(out_ref.at[part], out_hbm.at[part], sems.at[place]))
        copies[-1].start()
    for copy in copies:
        copy.wait()


def run_last(level, partial, own, other, basis_u):
    vmem, chunks = pl.BlockSpec(memory_space=pltpu.VMEM), 4
    return pl.pallas_call(
        functools.partial(last_kernel, level, chunks),
        out_shape=jax.ShapeDtypeStruct(partial.shape, F32),
        in_specs=[vmem] * 4,
        out_specs=pl.BlockSpec(memory_space=pl.ANY),
        scratch_shapes=[pltpu.VMEM(partial.shape, F32), pltpu.SemaphoreType.DMA((chunks,))],
        compiler_params=pltpu.CompilerParams(vmem_limit_bytes=2 * 2**20),
    )(partial, own, other, basis_u)


def run(kernel, outs, *args, after=(), flops=0):
    vmem, unread = pl.BlockSpec(memory_space=pltpu.VMEM), pl.BlockSpec(memory_space=pl.ANY)
    return pl.pallas_call(
        lambda *refs: kernel(*refs[: len(args)], *refs[len(args) + len(after) :]),
        out_shape=[jax.ShapeDtypeStruct(shape, F32) for shape in outs],
        in_specs=[vmem] * len(args) + [unread] * len(after),
        out_specs=[vmem] * len(outs),
        cost_estimate=pl.CostEstimate(flops=flops, bytes_accessed=0, transcendentals=0) if flops else None,
        compiler_params=pltpu.CompilerParams(vmem_limit_bytes=2 * 2**20),
    )(*args, *after)


def add_kernel(first_ref, second_ref, out_ref):
    out_ref[...] = first_ref[...] + second_ref[...]


def first_of_kernel(first_ref, second_ref, out_ref):
    out_ref[...] = first_ref[...] + second_ref[0]


def added(first, second, **options):
    return run(add_kernel, [first.shape], first, second, **options)[0]


def run_start(right_sides, basis_u, basis_v, coupling):
    columns, (points, rank) = right_sides.shape[1], basis_u.shape[1:]
    shape = jax.ShapeDtypeStruct
    arrays = [pltpu.with_memory_space_constraint(value, pltpu.HBM)
              for value in (right_sides, basis_u, basis_v, coupling)]
    outs = [shape((columns, points), F32), shape((columns, rank), F32), shape((points, rank), BF16),
            shape((points, rank), BF16), shape(coupling.shape[1:], BF16), shape((points, columns), F32)]
    return pl.pallas_call(
        start_kernel,
        out_shape=outs,
        in_specs=[pl.BlockSpec(memory_space=pl.ANY)] * len(arrays),
        out_specs=[pl.BlockSpec(memory_space=pltpu.VMEM)] * len(outs),
        scratch_shapes=[pltpu.VMEM((points, rank), BF16), pltpu.SemaphoreType.DMA((5,))],
        compiler_params=pltpu.CompilerParams(vmem_limit_bytes=4 * 2**20),
    )(*arrays)


def tied(value, *others):
    return lax.optimization_barrier((value,) + others)[0]


def traded(value, mask):
    if mask < lax.axis_size("sub"):
        return lax.ppermute(value, "sub", [(source, source ^ mask) for source in range(lax.axis_size("sub"))])
    devices = lax.axis_size("grp") * lax.axis_size("sub")
    return lax.ppermute(value, AXES, [(source, source ^ mask) for source in range(devices)])


def tree(right_sides, basis_u, basis_v, coupling):
    points, rank = basis_u.shape[1:]
    columns = right_sides.shape[1]
    half = columns // 2
    square, block, rows = (rank, rank), (half, rank), (rank // 2, rank)

    current, own, u_first, v_second, couple, right_near = run_start(right_sides, basis_u, basis_v, coupling)
    other = traded(own, 1)
    first_sum, first_cross = run(first_sum_kernel, [(columns, rank), square], current, u_first, v_second)
    weights0, keep, send = run(
        pair_kernel, [(columns, rank), block, block], own, other, couple, first_sum, first_cross
    )
    got = traded(send, 1)
    early, keep_cross, send_cross = run(
        cross_kernel, [(4,) + square, (2,) + rows, (2,) + rows], basis_u, basis_v, after=[weights0], flops=2 * 10**9
    )
    sums, sums_send = run(
        later_sums_kernel, [(3,) + block, (3,) + block], current, weights0, basis_u, basis_v,
        after=[keep_cross], flops=2 * 10**9,
    )
    sum1 = added(keep, got, after=[sums])

    across = traded(sum1, 2)
    cross_got = traded(tied(send_cross, sum1), 1)
    early_got = traded(tied(early, sum1), 1)
    sums_got = traded(tied(sums_send, sum1), 1)
    cross32, cross43 = run(mix_kernel, [rows, rows], keep_cross, cross_got, flops=2 * 10**9)
    cross32_across = traded(cross32, 2)
    cross43_across = traded(cross43, 4)
    (weights1,) = run(first_weights_kernel, [block], sum1, across, coupling, flops=8 * 10**9)
    second, pair = run(
        second_third_kernel, [block, (2,) + block], weights1, early, early_got, sums, sums_got
    )

    both, beside, across = traded(second, 6), traded(pair, 2), traded(second, 4)
    fourth, cross42 = run(
        fourth_kernel, [block, square], weights1, early, early_got, sums, sums_got, flops=800 * 10**6
    )
    cross32, cross43 = run(
        both_added_kernel, [rows, rows], cross32, cross32_across, cross43, cross43_across, after=[fourth]
    )
    cross32_got = traded(cross32, 1)
    (weights2,) = run(
        functools.partial(square_weights_kernel, 2, "sub", 2, 2), [block], second, beside, across, both, coupling,
        flops=8 * 10**9,
    )
    cross43_across = traded(cross43, 2)
    third, later4 = run(
        third_fourth_kernel, [block, block],
        weights2, cross32, cross32_got, pair, beside, fourth, cross42,
    )

    sum4 = added(later4, traded(later4, 2), after=[third])
    sum4_got = traded(sum4, 4)
    both, across, beside = traded(third, 12), traded(third, 8), traded(third, 4)
    cross43 = added(cross43, cross43_across, after=[third])
    cross43_got = traded(cross43, 1)
    (weights3,) = run(
        functools.partial(square_weights_kernel, 3, "sub", 3, 2), [block], third, beside, across, both, coupling
    )
    sum4 = added(sum4, sum4_got, after=[weights3], flops=8 * 10**9)
    (sum4,) = run(last_sum_kernel, [block], weights3, sum4, cross43, cross43_got)

    both, beside, across = traded(sum4, 24), traded(sum4, 8), traded(sum4, 16)
    (three,) = run(stack_kernel, [(3,) + block], weights1, weights2, weights3, after=[sum4])
    three_got = traded(three, 1)
    (partial,) = run(
        gather_kernel, [(points, columns)], right_near, basis_u, weights0, three, three_got, flops=2 * 10**9
    )
    own_sum = added(sum4, beside, after=[both], flops=4 * 10**9)
    (weights4,) = run(
        functools.partial(square_weights_kernel, 4, "grp", 0, 1), [block], own_sum, across, both, coupling
    )
    return run_last(4, partial, weights4, traded(weights4, 1), basis_u)


def solution(mesh):
    n_grp, n_sub = mesh.shape["grp"], mesh.shape["sub"]

    def per_device(right_sides, basis_u, basis_v, coupling):
        if basis_u.shape[0] == 5 and n_grp == 2 and n_sub == 16:
            return tree(right_sides, basis_u, basis_v, coupling)
        return bit_by_bit(right_sides, basis_u, basis_v, coupling)

    in_specs = (P(AXES, None), P(None, AXES, None), P(None, AXES, None), P(None, AXES, None))
    return jax.shard_map(
        per_device, mesh=mesh, in_specs=in_specs, out_specs=P(AXES, None), check_vma=False
    )
```

```python
import functools

import jax
import jax.numpy as jnp
from jax import lax
from jax.experimental import pallas as pl
from jax.experimental.pallas import tpu as pltpu
from jax.sharding import PartitionSpec as P

F32 = jnp.float32
BF16 = jnp.bfloat16
AXES = ("grp", "sub")


def swapped(value, axis, bit):
    mask = 2**bit
    pairs = [(source, source ^ mask) for source in range(lax.axis_size(axis))]
    return lax.ppermute(value, axis, pairs)


def partner(value, bit, sub_bits):
    if bit < sub_bits:
        return swapped(value, "sub", bit)
    return swapped(value, "grp", bit - sub_bits)


def pairwise(own_sum, first_bit, span_bits, sub_bits, lower_half):
    for bit in range(first_bit, span_bits):
        own_sum = own_sum + partner(own_sum, bit, sub_bits)
    other_sum = partner(own_sum, span_bits, sub_bits)
    first_half = jnp.where(lower_half, own_sum, other_sum)
    second_half = jnp.where(lower_half, other_sum, own_sum)
    return jnp.concatenate([first_half, second_half], axis=0)


def bit_by_bit(right_sides, basis_u, basis_v, coupling):
    highest = lax.Precision.HIGHEST
    sub_bits = lax.axis_size("sub").bit_length() - 1
    all_bits = sub_bits + lax.axis_size("grp").bit_length() - 1
    levels = basis_u.shape[0]
    position = lax.axis_index("grp") * lax.axis_size("sub") + lax.axis_index("sub")
    current = right_sides
    for height in range(levels):
        span_bits = all_bits - levels + height
        v_basis = basis_v[height].astype(F32)
        own_sum = jnp.einsum("pr,pn->rn", v_basis, current, precision=highest)
        lower_half = jnp.bitwise_and(jnp.right_shift(position, span_bits), 1) == 0
        node_sum = pairwise(own_sum, 0, span_bits, sub_bits, lower_half)
        weights = jnp.dot(coupling[height].astype(F32), node_sum, precision=highest)
        current = current - jnp.dot(basis_u[height].astype(F32), weights, precision=highest)
    return current


def split(value):
    high = value.astype(BF16)
    low = (value - high.astype(F32)).astype(BF16)
    return high, low


def stacked(value):
    return jnp.concatenate(split(value), axis=0)


def folded(value):
    half = value.shape[0] // 2
    return value[:half] + value[half:]


def dot(left, right):
    return lax.dot_general(left, right, (((1,), (0,)), ((), ())), preferred_element_type=F32)


def dot_transposed(left, right):
    return lax.dot_general(left, right, (((1,), (1,)), ((), ())), preferred_element_type=F32)


def weights_of(lower, upper, couple):
    rank = couple.shape[0]
    lower, upper = stacked(lower), stacked(upper)
    return folded(dot_transposed(lower, couple[:, :rank]) + dot_transposed(upper, couple[:, rank:]))


def correction(weights, cross):
    high, low = split(cross)
    both = stacked(weights)
    return folded(dot(both, high) + dot(both, low))


def bit_is_set(axis, bit):
    return jnp.bitwise_and(jnp.right_shift(lax.axis_index(axis), bit), 1) == 1


def ordered(flag, own, other):
    return jnp.where(flag, other, own), jnp.where(flag, own, other)


def start_kernel(right_hbm, u_hbm, v_hbm, c_hbm, current_ref, sum_ref, u_ref, v_ref, c_ref, right_ref,
                 first_ref, sems):
    sources = [right_hbm, v_hbm.at[0], v_hbm.at[1], u_hbm.at[0], c_hbm.at[0]]
    targets = [right_ref, first_ref, v_ref, u_ref, c_ref]
    copies = [pltpu.make_async_copy(*pair, sems.at[place]) for place, pair in enumerate(zip(sources, targets))]
    for copy in copies:
        copy.start()
    copies[0].wait()
    current = right_ref[...].T
    current_ref[...] = current
    copies[1].wait()
    sum_ref[...] = folded(dot(stacked(current), first_ref[...]))
    for copy in copies[2:]:
        copy.wait()


def first_sum_kernel(current_ref, u_ref, v_ref, sum_ref, cross_ref):
    sum_ref[...] = folded(dot(stacked(current_ref[...]), v_ref[...]))
    cross_ref[...] = dot(u_ref[...].T, v_ref[...])


def pair_kernel(own_ref, other_ref, c_ref, sum_ref, cross_ref, weights_ref, keep_ref, send_ref):
    upper_core = bit_is_set("sub", 0)
    half = keep_ref.shape[0]
    weights = weights_of(*ordered(upper_core, own_ref[...], other_ref[...]), c_ref[...])
    weights_ref[...] = weights
    later = sum_ref[...] - correction(weights, cross_ref[...])
    keep_ref[...], send_ref[...] = ordered(upper_core, later[:half], later[half:])


def later_sums_kernel(current_ref, weights_ref, u_ref, v_ref, keep_ref, send_ref):
    upper_core = bit_is_set("sub", 0)
    half = keep_ref.shape[1]
    current = current_ref[...] - folded(dot_transposed(stacked(weights_ref[...]), u_ref[0]))
    current = stacked(current)
    for place in range(keep_ref.shape[0]):
        later = folded(dot(current, v_ref[place + 2]))
        keep_ref[place], send_ref[place] = ordered(upper_core, later[:half], later[half:])


def cross_kernel(u_ref, v_ref, early_ref, keep_ref, send_ref):
    upper_core = bit_is_set("sub", 0)
    first, second, third = u_ref[1].T, u_ref[2].T, u_ref[3].T
    early_ref[0] = dot(first, v_ref[2])
    early_ref[1] = dot(first, v_ref[3])
    early_ref[2] = dot(first, v_ref[4])
    early_ref[3] = dot(second, v_ref[4])
    rows = keep_ref.shape[1]
    for place, cross in enumerate((dot(second, v_ref[3]), dot(third, v_ref[4]))):
        keep_ref[place], send_ref[place] = ordered(upper_core, cross[:rows], cross[rows:])


def mix_kernel(keep_ref, got_ref, third_ref, fourth_ref):
    third_ref[...], fourth_ref[...] = keep_ref[0] + got_ref[0], keep_ref[1] + got_ref[1]


def both_added_kernel(third_ref, third_got_ref, fourth_ref, fourth_got_ref, third_out_ref, fourth_out_ref):
    third_out_ref[...] = third_ref[...] + third_got_ref[...]
    fourth_out_ref[...] = fourth_ref[...] + fourth_got_ref[...]


def whole(half_ref, got_ref):
    return jnp.concatenate(ordered(bit_is_set("sub", 0), half_ref[...], got_ref[...]), axis=0)


def first_weights_kernel(own_ref, across_ref, c_ref, weights_ref):
    lower, upper = ordered(bit_is_set("sub", 1), own_ref[...], across_ref[...])
    weights_ref[...] = weights_of(lower, upper, c_ref[1])


def square_weights_kernel(level, axis, bit, own_count, *refs):
    *part_refs, c_ref, weights_ref = refs
    parts = [ref[0] if len(ref.shape) == 3 else ref[...] for ref in part_refs]
    own, other = sum(parts[1:own_count], parts[0]), sum(parts[own_count + 1 :], parts[own_count])
    weights_ref[...] = weights_of(*ordered(bit_is_set(axis, bit), own, other), c_ref[level])


def second_third_kernel(weights_ref, early_ref, got_ref, sums_ref, got_sums_ref, second_ref, pair_ref):
    weights = weights_ref[...]
    second_ref[...] = sums_ref[0] + got_sums_ref[0] - correction(weights, early_ref[0] + got_ref[0])
    pair_ref[0] = second_ref[...]
    pair_ref[1] = sums_ref[1] + got_sums_ref[1] - correction(weights, early_ref[1] + got_ref[1])


def fourth_kernel(weights_ref, early_ref, got_ref, sums_ref, got_sums_ref, fourth_ref, cross_ref):
    fourth_ref[...] = sums_ref[2] + got_sums_ref[2] - correction(weights_ref[...], early_ref[2] + got_ref[2])
    cross_ref[...] = early_ref[3] + got_ref[3]


def third_fourth_kernel(weights_ref, half_ref, half_got_ref, pair_ref, beside_ref, fourth_ref, cross_ref,
                        third_ref, later_ref):
    weights = weights_ref[...]
    cross = whole(half_ref, half_got_ref)
    third_ref[...] = pair_ref[1] + beside_ref[1] - correction(weights, cross)
    later_ref[...] = fourth_ref[...] - correction(weights, cross_ref[...])


def last_sum_kernel(weights_ref, sum_ref, half_ref, half_got_ref, later_ref):
    later_ref[...] = sum_ref[...] - correction(weights_ref[...], whole(half_ref, half_got_ref))


def stack_kernel(first_ref, second_ref, third_ref, out_ref):
    out_ref[0], out_ref[1], out_ref[2] = first_ref[...], second_ref[...], third_ref[...]


def columns_of(own, other):
    lower, upper = ordered(bit_is_set("sub", 0), own, other)
    return jnp.concatenate(split(jnp.concatenate([lower, upper], axis=0).T), axis=1)


def fold_columns(value):
    half = value.shape[1] // 2
    return value[:, :half] + value[:, half:]


def gather_kernel(right_ref, u_ref, first_ref, own_ref, other_ref, out_ref):
    total = dot(u_ref[0], jnp.concatenate(split(first_ref[...].T), axis=1))
    for place in range(own_ref.shape[0]):
        total = total + dot(u_ref[place + 1], columns_of(own_ref[place], other_ref[place]))
    out_ref[...] = right_ref[...] - fold_columns(total)


def last_kernel(level, chunks, partial_ref, own_ref, other_ref, u_ref, out_hbm, out_ref, sems):
    weights = columns_of(own_ref[...], other_ref[...])
    rows = out_ref.shape[0] // chunks
    copies = []
    for place in range(chunks):
        part = pl.ds(place * rows, rows)
        out_ref[part] = partial_ref[part] - fold_columns(dot(u_ref[level, part], weights))
        copies.append(pltpu.make_async_copy(out_ref.at[part], out_hbm.at[part], sems.at[place]))
        copies[-1].start()
    for copy in copies:
        copy.wait()


def run_last(level, partial, own, other, basis_u):
    vmem, chunks = pl.BlockSpec(memory_space=pltpu.VMEM), 4
    return pl.pallas_call(
        functools.partial(last_kernel, level, chunks),
        out_shape=jax.ShapeDtypeStruct(partial.shape, F32),
        in_specs=[vmem] * 4,
        out_specs=pl.BlockSpec(memory_space=pl.ANY),
        scratch_shapes=[pltpu.VMEM(partial.shape, F32), pltpu.SemaphoreType.DMA((chunks,))],
        compiler_params=pltpu.CompilerParams(vmem_limit_bytes=2 * 2**20),
    )(partial, own, other, basis_u)


def run(kernel, outs, *args, after=(), flops=0):
    vmem, unread = pl.BlockSpec(memory_space=pltpu.VMEM), pl.BlockSpec(memory_space=pl.ANY)
    return pl.pallas_call(
        lambda *refs: kernel(*refs[: len(args)], *refs[len(args) + len(after) :]),
        out_shape=[jax.ShapeDtypeStruct(shape, F32) for shape in outs],
        in_specs=[vmem] * len(args) + [unread] * len(after),
        out_specs=[vmem] * len(outs),
        cost_estimate=pl.CostEstimate(flops=flops, bytes_accessed=0, transcendentals=0) if flops else None,
        compiler_params=pltpu.CompilerParams(vmem_limit_bytes=2 * 2**20),
    )(*args, *after)


def add_kernel(first_ref, second_ref, out_ref):
    out_ref[...] = first_ref[...] + second_ref[...]


def first_of_kernel(first_ref, second_ref, out_ref):
    out_ref[...] = first_ref[...] + second_ref[0]


def added(first, second, **options):
    return run(add_kernel, [first.shape], first, second, **options)[0]


def run_start(right_sides, basis_u, basis_v, coupling):
    columns, (points, rank) = right_sides.shape[1], basis_u.shape[1:]
    shape = jax.ShapeDtypeStruct
    arrays = [pltpu.with_memory_space_constraint(value, pltpu.HBM)
              for value in (right_sides, basis_u, basis_v, coupling)]
    outs = [shape((columns, points), F32), shape((columns, rank), F32), shape((points, rank), BF16),
            shape((points, rank), BF16), shape(coupling.shape[1:], BF16), shape((points, columns), F32)]
    return pl.pallas_call(
        start_kernel,
        out_shape=outs,
        in_specs=[pl.BlockSpec(memory_space=pl.ANY)] * len(arrays),
        out_specs=[pl.BlockSpec(memory_space=pltpu.VMEM)] * len(outs),
        scratch_shapes=[pltpu.VMEM((points, rank), BF16), pltpu.SemaphoreType.DMA((5,))],
        compiler_params=pltpu.CompilerParams(vmem_limit_bytes=4 * 2**20),
    )(*arrays)


def tied(value, *others):
    return lax.optimization_barrier((value,) + others)[0]


def traded(value, mask):
    if mask < lax.axis_size("sub"):
        return lax.ppermute(value, "sub", [(source, source ^ mask) for source in range(lax.axis_size("sub"))])
    devices = lax.axis_size("grp") * lax.axis_size("sub")
    return lax.ppermute(value, AXES, [(source, source ^ mask) for source in range(devices)])


def tree(right_sides, basis_u, basis_v, coupling):
    points, rank = basis_u.shape[1:]
    columns = right_sides.shape[1]
    half = columns // 2
    square, block, rows = (rank, rank), (half, rank), (rank // 2, rank)

    current, own, u_first, v_second, couple, right_near = run_start(right_sides, basis_u, basis_v, coupling)
    other = traded(own, 1)
    first_sum, first_cross = run(first_sum_kernel, [(columns, rank), square], current, u_first, v_second)
    weights0, keep, send = run(
        pair_kernel, [(columns, rank), block, block], own, other, couple, first_sum, first_cross
    )
    got = traded(send, 1)
    early, keep_cross, send_cross = run(
        cross_kernel, [(4,) + square, (2,) + rows, (2,) + rows], basis_u, basis_v, after=[weights0], flops=2 * 10**9
    )
    sum1 = added(keep, got, after=[keep_cross])
    sums, sums_send = run(
        later_sums_kernel, [(3,) + block, (3,) + block], current, weights0, basis_u, basis_v,
        after=[sum1], flops=2 * 10**9,
    )

    across = traded(sum1, 2)
    cross_got = traded(tied(send_cross, sum1), 1)
    early_got = traded(tied(early, sum1), 1)
    sums_got = traded(sums_send, 1)
    cross32, cross43 = run(mix_kernel, [rows, rows], keep_cross, cross_got, flops=2 * 10**9)
    cross32_across = traded(cross32, 2)
    cross43_across = traded(cross43, 4)
    (weights1,) = run(first_weights_kernel, [block], sum1, across, coupling, flops=8 * 10**9)
    second, pair = run(
        second_third_kernel, [block, (2,) + block], weights1, early, early_got, sums, sums_got
    )

    both, beside, across = traded(second, 6), traded(pair, 2), traded(second, 4)
    fourth, cross42 = run(
        fourth_kernel, [block, square], weights1, early, early_got, sums, sums_got, flops=800 * 10**6
    )
    cross32, cross43 = run(
        both_added_kernel, [rows, rows], cross32, cross32_across, cross43, cross43_across, after=[fourth]
    )
    cross32_got = traded(cross32, 1)
    (weights2,) = run(
        functools.partial(square_weights_kernel, 2, "sub", 2, 2), [block], second, beside, across, both, coupling,
        flops=8 * 10**9,
    )
    cross43_across = traded(cross43, 2)
    third, later4 = run(
        third_fourth_kernel, [block, block],
        weights2, cross32, cross32_got, pair, beside, fourth, cross42,
    )

    sum4 = added(later4, traded(later4, 2), after=[third])
    sum4_got = traded(sum4, 4)
    both, across, beside = traded(third, 12), traded(third, 8), traded(third, 4)
    cross43 = added(cross43, cross43_across, after=[third])
    cross43_got = traded(cross43, 1)
    (weights3,) = run(
        functools.partial(square_weights_kernel, 3, "sub", 3, 2), [block], third, beside, across, both, coupling
    )
    sum4 = added(sum4, sum4_got, after=[weights3], flops=8 * 10**9)
    (sum4,) = run(last_sum_kernel, [block], weights3, sum4, cross43, cross43_got)

    both, beside, across = traded(sum4, 24), traded(sum4, 8), traded(sum4, 16)
    (three,) = run(stack_kernel, [(3,) + block], weights1, weights2, weights3, after=[sum4])
    three_got = traded(three, 1)
    (partial,) = run(
        gather_kernel, [(points, columns)], right_near, basis_u, weights0, three, three_got, flops=2 * 10**9
    )
    own_sum = added(sum4, beside, after=[both], flops=4 * 10**9)
    (weights4,) = run(
        functools.partial(square_weights_kernel, 4, "grp", 0, 1), [block], own_sum, across, both, coupling
    )
    return run_last(4, partial, weights4, traded(weights4, 1), basis_u)


def solution(mesh):
    n_grp, n_sub = mesh.shape["grp"], mesh.shape["sub"]

    def per_device(right_sides, basis_u, basis_v, coupling):
        if basis_u.shape[0] == 5 and n_grp == 2 and n_sub == 16:
            return tree(right_sides, basis_u, basis_v, coupling)
        return bit_by_bit(right_sides, basis_u, basis_v, coupling)

    in_specs = (P(AXES, None), P(None, AXES, None), P(None, AXES, None), P(None, AXES, None))
    return jax.shard_map(
        per_device, mesh=mesh, in_specs=in_specs, out_specs=P(AXES, None), check_vma=False
    )
```

```python
import functools

import jax
import jax.numpy as jnp
from jax import lax
from jax.experimental import pallas as pl
from jax.experimental.pallas import tpu as pltpu
from jax.sharding import PartitionSpec as P

F32 = jnp.float32
BF16 = jnp.bfloat16
AXES = ("grp", "sub")


def swapped(value, axis, bit):
    mask = 2**bit
    pairs = [(source, source ^ mask) for source in range(lax.axis_size(axis))]
    return lax.ppermute(value, axis, pairs)


def partner(value, bit, sub_bits):
    if bit < sub_bits:
        return swapped(value, "sub", bit)
    return swapped(value, "grp", bit - sub_bits)


def pairwise(own_sum, first_bit, span_bits, sub_bits, lower_half):
    for bit in range(first_bit, span_bits):
        own_sum = own_sum + partner(own_sum, bit, sub_bits)
    other_sum = partner(own_sum, span_bits, sub_bits)
    first_half = jnp.where(lower_half, own_sum, other_sum)
    second_half = jnp.where(lower_half, other_sum, own_sum)
    return jnp.concatenate([first_half, second_half], axis=0)


def bit_by_bit(right_sides, basis_u, basis_v, coupling):
    highest = lax.Precision.HIGHEST
    sub_bits = lax.axis_size("sub").bit_length() - 1
    all_bits = sub_bits + lax.axis_size("grp").bit_length() - 1
    levels = basis_u.shape[0]
    position = lax.axis_index("grp") * lax.axis_size("sub") + lax.axis_index("sub")
    current = right_sides
    for height in range(levels):
        span_bits = all_bits - levels + height
        v_basis = basis_v[height].astype(F32)
        own_sum = jnp.einsum("pr,pn->rn", v_basis, current, precision=highest)
        lower_half = jnp.bitwise_and(jnp.right_shift(position, span_bits), 1) == 0
        node_sum = pairwise(own_sum, 0, span_bits, sub_bits, lower_half)
        weights = jnp.dot(coupling[height].astype(F32), node_sum, precision=highest)
        current = current - jnp.dot(basis_u[height].astype(F32), weights, precision=highest)
    return current


def split(value):
    high = value.astype(BF16)
    low = (value - high.astype(F32)).astype(BF16)
    return high, low


def stacked(value):
    return jnp.concatenate(split(value), axis=0)


def folded(value):
    half = value.shape[0] // 2
    return value[:half] + value[half:]


def dot(left, right):
    return lax.dot_general(left, right, (((1,), (0,)), ((), ())), preferred_element_type=F32)


def dot_transposed(left, right):
    return lax.dot_general(left, right, (((1,), (1,)), ((), ())), preferred_element_type=F32)


def weights_of(lower, upper, couple):
    rank = couple.shape[0]
    lower, upper = stacked(lower), stacked(upper)
    return folded(dot_transposed(lower, couple[:, :rank]) + dot_transposed(upper, couple[:, rank:]))


def correction(weights, cross):
    high, low = split(cross)
    both = stacked(weights)
    return folded(dot(both, high) + dot(both, low))


def bit_is_set(axis, bit):
    return jnp.bitwise_and(jnp.right_shift(lax.axis_index(axis), bit), 1) == 1


def ordered(flag, own, other):
    return jnp.where(flag, other, own), jnp.where(flag, own, other)


def start_kernel(right_hbm, u_hbm, v_hbm, c_hbm, current_ref, sum_ref, u_ref, v_ref, c_ref, right_ref,
                 first_ref, sems):
    sources = [right_hbm, v_hbm.at[0], v_hbm.at[1], u_hbm.at[0], c_hbm.at[0]]
    targets = [right_ref, first_ref, v_ref, u_ref, c_ref]
    copies = [pltpu.make_async_copy(*pair, sems.at[place]) for place, pair in enumerate(zip(sources, targets))]
    for copy in copies:
        copy.start()
    copies[0].wait()
    current = right_ref[...].T
    current_ref[...] = current
    copies[1].wait()
    sum_ref[...] = folded(dot(stacked(current), first_ref[...]))
    for copy in copies[2:]:
        copy.wait()


def effect(couple, cross):
    high, low = split(cross)
    couple = couple.T
    return dot(couple, high) + dot(couple, low)


def first_sum_kernel(current_ref, u_ref, v_ref, c_ref, sum_ref, effect_ref):
    sum_ref[...] = folded(dot(stacked(current_ref[...]), v_ref[...]))
    effect_ref[...] = effect(c_ref[...], dot(u_ref[...].T, v_ref[...]))


def pair_kernel(own_ref, other_ref, sum_ref, effect_ref, keep_ref, send_ref):
    upper_core = bit_is_set("sub", 0)
    half = keep_ref.shape[0]
    node = jnp.concatenate(ordered(upper_core, own_ref[...], other_ref[...]), axis=1)
    later = sum_ref[...] - correction(node, effect_ref[...])
    keep_ref[...], send_ref[...] = ordered(upper_core, later[:half], later[half:])


def pair_weights_kernel(own_ref, other_ref, c_ref, weights_ref):
    weights_ref[...] = weights_of(*ordered(bit_is_set("sub", 0), own_ref[...], other_ref[...]), c_ref[...])


def later_sums_kernel(current_ref, weights_ref, u_ref, v_ref, keep_ref, send_ref):
    upper_core = bit_is_set("sub", 0)
    half = keep_ref.shape[1]
    current = current_ref[...] - folded(dot_transposed(stacked(weights_ref[...]), u_ref[...]))
    current = stacked(current)
    for place in range(keep_ref.shape[0]):
        later = folded(dot(current, v_ref[place + 2]))
        keep_ref[place], send_ref[place] = ordered(upper_core, later[:half], later[half:])


def cross_kernel(u_ref, v_ref, early_ref, keep_ref, send_ref):
    upper_core = bit_is_set("sub", 0)
    first, second, third = u_ref[1].T, u_ref[2].T, u_ref[3].T
    early_ref[0] = dot(first, v_ref[2])
    early_ref[1] = dot(first, v_ref[3])
    early_ref[2] = dot(first, v_ref[4])
    early_ref[3] = dot(second, v_ref[4])
    rows = keep_ref.shape[1]
    for place, cross in enumerate((dot(second, v_ref[3]), dot(third, v_ref[4]))):
        keep_ref[place], send_ref[place] = ordered(upper_core, cross[:rows], cross[rows:])


def mix_kernel(keep_ref, got_ref, third_ref, fourth_ref):
    third_ref[...], fourth_ref[...] = keep_ref[0] + got_ref[0], keep_ref[1] + got_ref[1]


def both_added_kernel(third_ref, third_got_ref, fourth_ref, fourth_got_ref, third_out_ref, fourth_out_ref):
    third_out_ref[...] = third_ref[...] + third_got_ref[...]
    fourth_out_ref[...] = fourth_ref[...] + fourth_got_ref[...]


def whole(half_ref, got_ref):
    return jnp.concatenate(ordered(bit_is_set("sub", 0), half_ref[...], got_ref[...]), axis=0)


def first_weights_kernel(own_ref, across_ref, c_ref, weights_ref):
    lower, upper = ordered(bit_is_set("sub", 1), own_ref[...], across_ref[...])
    weights_ref[...] = weights_of(lower, upper, c_ref[1])


def square_weights_kernel(level, axis, bit, own_count, *refs):
    *part_refs, c_ref, weights_ref = refs
    parts = [ref[0] if len(ref.shape) == 3 else ref[...] for ref in part_refs]
    own, other = sum(parts[1:own_count], parts[0]), sum(parts[own_count + 1 :], parts[own_count])
    weights_ref[...] = weights_of(*ordered(bit_is_set(axis, bit), own, other), c_ref[level])


def second_third_kernel(weights_ref, early_ref, got_ref, sums_ref, got_sums_ref, second_ref, pair_ref):
    weights = weights_ref[...]
    second_ref[...] = sums_ref[0] + got_sums_ref[0] - correction(weights, early_ref[0] + got_ref[0])
    pair_ref[0] = second_ref[...]
    pair_ref[1] = sums_ref[1] + got_sums_ref[1] - correction(weights, early_ref[1] + got_ref[1])


def fourth_kernel(weights_ref, early_ref, got_ref, sums_ref, got_sums_ref, fourth_ref, cross_ref):
    fourth_ref[...] = sums_ref[2] + got_sums_ref[2] - correction(weights_ref[...], early_ref[2] + got_ref[2])
    cross_ref[...] = early_ref[3] + got_ref[3]


def third_fourth_kernel(weights_ref, half_ref, half_got_ref, pair_ref, beside_ref, fourth_ref, cross_ref,
                        third_ref, later_ref):
    weights = weights_ref[...]
    cross = whole(half_ref, half_got_ref)
    third_ref[...] = pair_ref[1] + beside_ref[1] - correction(weights, cross)
    later_ref[...] = fourth_ref[...] - correction(weights, cross_ref[...])


def last_sum_kernel(weights_ref, sum_ref, half_ref, half_got_ref, later_ref):
    later_ref[...] = sum_ref[...] - correction(weights_ref[...], whole(half_ref, half_got_ref))


def stack_kernel(first_ref, second_ref, third_ref, out_ref):
    out_ref[0], out_ref[1], out_ref[2] = first_ref[...], second_ref[...], third_ref[...]


def columns_of(own, other):
    lower, upper = ordered(bit_is_set("sub", 0), own, other)
    return jnp.concatenate(split(jnp.concatenate([lower, upper], axis=0).T), axis=1)


def fold_columns(value):
    half = value.shape[1] // 2
    return value[:, :half] + value[:, half:]


def gather_kernel(right_ref, u_ref, first_ref, own_ref, other_ref, out_ref):
    total = dot(u_ref[0], jnp.concatenate(split(first_ref[...].T), axis=1))
    for place in range(own_ref.shape[0]):
        total = total + dot(u_ref[place + 1], columns_of(own_ref[place], other_ref[place]))
    out_ref[...] = right_ref[...] - fold_columns(total)


def last_kernel(level, chunks, partial_ref, own_ref, other_ref, u_ref, out_hbm, out_ref, sems):
    weights = columns_of(own_ref[...], other_ref[...])
    rows = out_ref.shape[0] // chunks
    copies = []
    for place in range(chunks):
        part = pl.ds(place * rows, rows)
        out_ref[part] = partial_ref[part] - fold_columns(dot(u_ref[level, part], weights))
        copies.append(pltpu.make_async_copy(out_ref.at[part], out_hbm.at[part], sems.at[place]))
        copies[-1].start()
    for copy in copies:
        copy.wait()


def run_last(level, partial, own, other, basis_u):
    vmem, chunks = pl.BlockSpec(memory_space=pltpu.VMEM), 4
    return pl.pallas_call(
        functools.partial(last_kernel, level, chunks),
        out_shape=jax.ShapeDtypeStruct(partial.shape, F32),
        in_specs=[vmem] * 4,
        out_specs=pl.BlockSpec(memory_space=pl.ANY),
        scratch_shapes=[pltpu.VMEM(partial.shape, F32), pltpu.SemaphoreType.DMA((chunks,))],
        compiler_params=pltpu.CompilerParams(vmem_limit_bytes=2 * 2**20),
    )(partial, own, other, basis_u)


def run(kernel, outs, *args, after=(), flops=0):
    vmem, unread = pl.BlockSpec(memory_space=pltpu.VMEM), pl.BlockSpec(memory_space=pl.ANY)
    return pl.pallas_call(
        lambda *refs: kernel(*refs[: len(args)], *refs[len(args) + len(after) :]),
        out_shape=[jax.ShapeDtypeStruct(shape, F32) for shape in outs],
        in_specs=[vmem] * len(args) + [unread] * len(after),
        out_specs=[vmem] * len(outs),
        cost_estimate=pl.CostEstimate(flops=flops, bytes_accessed=0, transcendentals=0) if flops else None,
        compiler_params=pltpu.CompilerParams(vmem_limit_bytes=2 * 2**20),
    )(*args, *after)


def add_kernel(first_ref, second_ref, out_ref):
    out_ref[...] = first_ref[...] + second_ref[...]


def first_of_kernel(first_ref, second_ref, out_ref):
    out_ref[...] = first_ref[...] + second_ref[0]


def added(first, second, **options):
    return run(add_kernel, [first.shape], first, second, **options)[0]


def run_start(right_sides, basis_u, basis_v, coupling):
    columns, (points, rank) = right_sides.shape[1], basis_u.shape[1:]
    shape = jax.ShapeDtypeStruct
    arrays = [pltpu.with_memory_space_constraint(value, pltpu.HBM)
              for value in (right_sides, basis_u, basis_v, coupling)]
    outs = [shape((columns, points), F32), shape((columns, rank), F32), shape((points, rank), BF16),
            shape((points, rank), BF16), shape(coupling.shape[1:], BF16), shape((points, columns), F32)]
    return pl.pallas_call(
        start_kernel,
        out_shape=outs,
        in_specs=[pl.BlockSpec(memory_space=pl.ANY)] * len(arrays),
        out_specs=[pl.BlockSpec(memory_space=pltpu.VMEM)] * len(outs),
        scratch_shapes=[pltpu.VMEM((points, rank), BF16), pltpu.SemaphoreType.DMA((5,))],
        compiler_params=pltpu.CompilerParams(vmem_limit_bytes=4 * 2**20),
    )(*arrays)


def tied(value, *others):
    return lax.optimization_barrier((value,) + others)[0]


def traded(value, mask):
    if mask < lax.axis_size("sub"):
        return lax.ppermute(value, "sub", [(source, source ^ mask) for source in range(lax.axis_size("sub"))])
    devices = lax.axis_size("grp") * lax.axis_size("sub")
    return lax.ppermute(value, AXES, [(source, source ^ mask) for source in range(devices)])


def tree(right_sides, basis_u, basis_v, coupling):
    points, rank = basis_u.shape[1:]
    columns = right_sides.shape[1]
    half = columns // 2
    square, block, rows = (rank, rank), (half, rank), (rank // 2, rank)

    current, own, u_first, v_second, couple, right_near = run_start(right_sides, basis_u, basis_v, coupling)
    other = traded(own, 1)
    first_sum, first_effect = run(
        first_sum_kernel, [(columns, rank), (2 * rank, rank)], current, u_first, v_second, couple
    )
    keep, send = run(pair_kernel, [block, block], own, other, first_sum, first_effect)
    got = traded(send, 1)
    early, keep_cross, send_cross = run(
        cross_kernel, [(4,) + square, (2,) + rows, (2,) + rows], basis_u, basis_v, after=[keep], flops=2 * 10**9
    )
    sum1 = added(keep, got, after=[keep_cross])
    (weights0,) = run(pair_weights_kernel, [(columns, rank)], own, other, couple, after=[sum1])
    sums, sums_send = run(
        later_sums_kernel, [(3,) + block, (3,) + block], current, weights0, u_first, basis_v, flops=2 * 10**9
    )

    across = traded(sum1, 2)
    cross_got = traded(tied(send_cross, sum1), 1)
    early_got = traded(tied(early, sum1), 1)
    sums_got = traded(sums_send, 1)
    cross32, cross43 = run(mix_kernel, [rows, rows], keep_cross, cross_got, flops=2 * 10**9)
    cross32_across = traded(cross32, 2)
    cross43_across = traded(cross43, 4)
    (weights1,) = run(first_weights_kernel, [block], sum1, across, coupling, flops=8 * 10**9)
    second, pair = run(
        second_third_kernel, [block, (2,) + block], weights1, early, early_got, sums, sums_got
    )

    both, beside, across = traded(second, 6), traded(pair, 2), traded(second, 4)
    fourth, cross42 = run(
        fourth_kernel, [block, square], weights1, early, early_got, sums, sums_got, flops=800 * 10**6
    )
    cross32, cross43 = run(
        both_added_kernel, [rows, rows], cross32, cross32_across, cross43, cross43_across, after=[fourth]
    )
    cross32_got = traded(cross32, 1)
    (weights2,) = run(
        functools.partial(square_weights_kernel, 2, "sub", 2, 2), [block], second, beside, across, both, coupling,
        flops=8 * 10**9,
    )
    cross43_across = traded(cross43, 2)
    third, later4 = run(
        third_fourth_kernel, [block, block],
        weights2, cross32, cross32_got, pair, beside, fourth, cross42,
    )

    sum4 = added(later4, traded(later4, 2), after=[third])
    sum4_got = traded(sum4, 4)
    both, across, beside = traded(third, 12), traded(third, 8), traded(third, 4)
    cross43 = added(cross43, cross43_across, after=[third])
    cross43_got = traded(cross43, 1)
    (weights3,) = run(
        functools.partial(square_weights_kernel, 3, "sub", 3, 2), [block], third, beside, across, both, coupling
    )
    sum4 = added(sum4, sum4_got, after=[weights3], flops=8 * 10**9)
    (sum4,) = run(last_sum_kernel, [block], weights3, sum4, cross43, cross43_got)

    both, beside, across = traded(sum4, 24), traded(sum4, 8), traded(sum4, 16)
    (three,) = run(stack_kernel, [(3,) + block], weights1, weights2, weights3, after=[sum4])
    three_got = traded(three, 1)
    (partial,) = run(
        gather_kernel, [(points, columns)], right_near, basis_u, weights0, three, three_got, flops=2 * 10**9
    )
    own_sum = added(sum4, beside, after=[both], flops=4 * 10**9)
    (weights4,) = run(
        functools.partial(square_weights_kernel, 4, "grp", 0, 1), [block], own_sum, across, both, coupling
    )
    return run_last(4, partial, weights4, traded(weights4, 1), basis_u)


def solution(mesh):
    n_grp, n_sub = mesh.shape["grp"], mesh.shape["sub"]

    def per_device(right_sides, basis_u, basis_v, coupling):
        if basis_u.shape[0] == 5 and n_grp == 2 and n_sub == 16:
            return tree(right_sides, basis_u, basis_v, coupling)
        return bit_by_bit(right_sides, basis_u, basis_v, coupling)

    in_specs = (P(AXES, None), P(None, AXES, None), P(None, AXES, None), P(None, AXES, None))
    return jax.shard_map(
        per_device, mesh=mesh, in_specs=in_specs, out_specs=P(AXES, None), check_vma=False
    )
```

```python
import functools

import jax
import jax.numpy as jnp
from jax import lax
from jax.experimental import pallas as pl
from jax.experimental.pallas import tpu as pltpu
from jax.sharding import PartitionSpec as P

F32 = jnp.float32
BF16 = jnp.bfloat16
AXES = ("grp", "sub")


def swapped(value, axis, bit):
    mask = 2**bit
    pairs = [(source, source ^ mask) for source in range(lax.axis_size(axis))]
    return lax.ppermute(value, axis, pairs)


def partner(value, bit, sub_bits):
    if bit < sub_bits:
        return swapped(value, "sub", bit)
    return swapped(value, "grp", bit - sub_bits)


def pairwise(own_sum, first_bit, span_bits, sub_bits, lower_half):
    for bit in range(first_bit, span_bits):
        own_sum = own_sum + partner(own_sum, bit, sub_bits)
    other_sum = partner(own_sum, span_bits, sub_bits)
    first_half = jnp.where(lower_half, own_sum, other_sum)
    second_half = jnp.where(lower_half, other_sum, own_sum)
    return jnp.concatenate([first_half, second_half], axis=0)


def bit_by_bit(right_sides, basis_u, basis_v, coupling):
    highest = lax.Precision.HIGHEST
    sub_bits = lax.axis_size("sub").bit_length() - 1
    all_bits = sub_bits + lax.axis_size("grp").bit_length() - 1
    levels = basis_u.shape[0]
    position = lax.axis_index("grp") * lax.axis_size("sub") + lax.axis_index("sub")
    current = right_sides
    for height in range(levels):
        span_bits = all_bits - levels + height
        v_basis = basis_v[height].astype(F32)
        own_sum = jnp.einsum("pr,pn->rn", v_basis, current, precision=highest)
        lower_half = jnp.bitwise_and(jnp.right_shift(position, span_bits), 1) == 0
        node_sum = pairwise(own_sum, 0, span_bits, sub_bits, lower_half)
        weights = jnp.dot(coupling[height].astype(F32), node_sum, precision=highest)
        current = current - jnp.dot(basis_u[height].astype(F32), weights, precision=highest)
    return current


def split(value):
    high = value.astype(BF16)
    low = (value - high.astype(F32)).astype(BF16)
    return high, low


def stacked(value):
    return jnp.concatenate(split(value), axis=0)


def folded(value):
    half = value.shape[0] // 2
    return value[:half] + value[half:]


def dot(left, right):
    return lax.dot_general(left, right, (((1,), (0,)), ((), ())), preferred_element_type=F32)


def dot_transposed(left, right):
    return lax.dot_general(left, right, (((1,), (1,)), ((), ())), preferred_element_type=F32)


def weights_of(lower, upper, couple):
    rank = couple.shape[0]
    lower, upper = stacked(lower), stacked(upper)
    return folded(dot_transposed(lower, couple[:, :rank]) + dot_transposed(upper, couple[:, rank:]))


def correction(weights, cross):
    high, low = split(cross)
    both = stacked(weights)
    return folded(dot(both, high) + dot(both, low))


def bit_is_set(axis, bit):
    return jnp.bitwise_and(jnp.right_shift(lax.axis_index(axis), bit), 1) == 1


def ordered(flag, own, other):
    return jnp.where(flag, other, own), jnp.where(flag, own, other)


def start_kernel(right_hbm, u_hbm, v_hbm, c_hbm, current_ref, sum_ref, u_ref, v_ref, c_ref, right_ref,
                 first_ref, sems):
    sources = [right_hbm, v_hbm.at[0], v_hbm.at[1], u_hbm.at[0], c_hbm.at[0]]
    targets = [right_ref, first_ref, v_ref, u_ref, c_ref]
    copies = [pltpu.make_async_copy(*pair, sems.at[place]) for place, pair in enumerate(zip(sources, targets))]
    for copy in copies:
        copy.start()
    copies[0].wait()
    current = right_ref[...].T
    current_ref[...] = current
    copies[1].wait()
    sum_ref[...] = folded(dot(stacked(current), first_ref[...]))
    for copy in copies[2:]:
        copy.wait()


def first_sum_kernel(current_ref, u_ref, v_ref, sum_ref, cross_ref):
    sum_ref[...] = folded(dot(stacked(current_ref[...]), v_ref[...]))
    cross_ref[...] = dot(u_ref[...].T, v_ref[...])


def pair_kernel(own_ref, other_ref, c_ref, sum_ref, cross_ref, weights_ref, keep_ref, send_ref):
    upper_core = bit_is_set("sub", 0)
    half = keep_ref.shape[0]
    weights = weights_of(*ordered(upper_core, own_ref[...], other_ref[...]), c_ref[...])
    weights_ref[...] = weights
    later = sum_ref[...] - correction(weights, cross_ref[...])
    keep_ref[...], send_ref[...] = ordered(upper_core, later[:half], later[half:])


def later_sums_kernel(current_ref, weights_ref, u_ref, v_ref, keep_ref, send_ref):
    upper_core = bit_is_set("sub", 0)
    half = keep_ref.shape[1]
    current = current_ref[...] - folded(dot_transposed(stacked(weights_ref[...]), u_ref[0]))
    current = stacked(current)
    for place in range(keep_ref.shape[0]):
        later = folded(dot(current, v_ref[place + 2]))
        keep_ref[place], send_ref[place] = ordered(upper_core, later[:half], later[half:])


def cross_kernel(u_ref, v_ref, early_ref, keep_ref, send_ref):
    upper_core = bit_is_set("sub", 0)
    first, second, third = u_ref[1].T, u_ref[2].T, u_ref[3].T
    early_ref[0] = dot(first, v_ref[2])
    early_ref[1] = dot(first, v_ref[3])
    early_ref[2] = dot(first, v_ref[4])
    early_ref[3] = dot(second, v_ref[4])
    rows = keep_ref.shape[1]
    for place, cross in enumerate((dot(second, v_ref[3]), dot(third, v_ref[4]))):
        keep_ref[place], send_ref[place] = ordered(upper_core, cross[:rows], cross[rows:])


def mix_kernel(keep_ref, got_ref, third_ref, fourth_ref):
    third_ref[...], fourth_ref[...] = keep_ref[0] + got_ref[0], keep_ref[1] + got_ref[1]


def both_added_kernel(third_ref, third_got_ref, fourth_ref, fourth_got_ref, third_out_ref, fourth_out_ref):
    third_out_ref[...] = third_ref[...] + third_got_ref[...]
    fourth_out_ref[...] = fourth_ref[...] + fourth_got_ref[...]


def whole(half_ref, got_ref):
    return jnp.concatenate(ordered(bit_is_set("sub", 0), half_ref[...], got_ref[...]), axis=0)


def first_weights_kernel(own_ref, across_ref, c_ref, weights_ref):
    lower, upper = ordered(bit_is_set("sub", 1), own_ref[...], across_ref[...])
    weights_ref[...] = weights_of(lower, upper, c_ref[1])


def square_weights_kernel(level, axis, bit, own_count, *refs):
    *part_refs, c_ref, weights_ref = refs
    parts = [ref[0] if len(ref.shape) == 3 else ref[...] for ref in part_refs]
    own, other = sum(parts[1:own_count], parts[0]), sum(parts[own_count + 1 :], parts[own_count])
    weights_ref[...] = weights_of(*ordered(bit_is_set(axis, bit), own, other), c_ref[level])


def second_third_kernel(weights_ref, early_ref, got_ref, sums_ref, got_sums_ref, second_ref, pair_ref):
    weights = weights_ref[...]
    second_ref[...] = sums_ref[0] + got_sums_ref[0] - correction(weights, early_ref[0] + got_ref[0])
    pair_ref[0] = second_ref[...]
    pair_ref[1] = sums_ref[1] + got_sums_ref[1] - correction(weights, early_ref[1] + got_ref[1])


def fourth_kernel(weights_ref, early_ref, got_ref, sums_ref, got_sums_ref, fourth_ref, cross_ref):
    fourth_ref[...] = sums_ref[2] + got_sums_ref[2] - correction(weights_ref[...], early_ref[2] + got_ref[2])
    cross_ref[...] = early_ref[3] + got_ref[3]


def third_fourth_kernel(weights_ref, half_ref, half_got_ref, pair_ref, beside_ref, fourth_ref, cross_ref,
                        third_ref, later_ref):
    weights = weights_ref[...]
    cross = whole(half_ref, half_got_ref)
    third_ref[...] = pair_ref[1] + beside_ref[1] - correction(weights, cross)
    later_ref[...] = fourth_ref[...] - correction(weights, cross_ref[...])


def last_sum_kernel(weights_ref, sum_ref, half_ref, half_got_ref, later_ref):
    later_ref[...] = sum_ref[...] - correction(weights_ref[...], whole(half_ref, half_got_ref))


def stack_kernel(first_ref, second_ref, third_ref, out_ref):
    out_ref[0], out_ref[1], out_ref[2] = first_ref[...], second_ref[...], third_ref[...]


def columns_of(own, other):
    lower, upper = ordered(bit_is_set("sub", 0), own, other)
    return jnp.concatenate(split(jnp.concatenate([lower, upper], axis=0).T), axis=1)


def fold_columns(value):
    half = value.shape[1] // 2
    return value[:, :half] + value[:, half:]


def gather_kernel(right_ref, u_ref, first_ref, own_ref, other_ref, out_ref):
    total = dot(u_ref[0], jnp.concatenate(split(first_ref[...].T), axis=1))
    for place in range(own_ref.shape[0]):
        total = total + dot(u_ref[place + 1], columns_of(own_ref[place], other_ref[place]))
    out_ref[...] = right_ref[...] - fold_columns(total)


def last_kernel(level, chunks, partial_ref, own_ref, other_ref, u_ref, out_hbm, out_ref, sems):
    weights = columns_of(own_ref[...], other_ref[...])
    rows = out_ref.shape[0] // chunks
    copies = []
    for place in range(chunks):
        part = pl.ds(place * rows, rows)
        out_ref[part] = partial_ref[part] - fold_columns(dot(u_ref[level, part], weights))
        copies.append(pltpu.make_async_copy(out_ref.at[part], out_hbm.at[part], sems.at[place]))
        copies[-1].start()
    for copy in copies:
        copy.wait()


def run_last(level, partial, own, other, basis_u):
    vmem, chunks = pl.BlockSpec(memory_space=pltpu.VMEM), 4
    return pl.pallas_call(
        functools.partial(last_kernel, level, chunks),
        out_shape=jax.ShapeDtypeStruct(partial.shape, F32),
        in_specs=[vmem] * 4,
        out_specs=pl.BlockSpec(memory_space=pl.ANY),
        scratch_shapes=[pltpu.VMEM(partial.shape, F32), pltpu.SemaphoreType.DMA((chunks,))],
        compiler_params=pltpu.CompilerParams(vmem_limit_bytes=2 * 2**20),
    )(partial, own, other, basis_u)


def run(kernel, outs, *args, after=(), flops=0):
    vmem, unread = pl.BlockSpec(memory_space=pltpu.VMEM), pl.BlockSpec(memory_space=pl.ANY)
    return pl.pallas_call(
        lambda *refs: kernel(*refs[: len(args)], *refs[len(args) + len(after) :]),
        out_shape=[jax.ShapeDtypeStruct(shape, F32) for shape in outs],
        in_specs=[vmem] * len(args) + [unread] * len(after),
        out_specs=[vmem] * len(outs),
        cost_estimate=pl.CostEstimate(flops=flops, bytes_accessed=0, transcendentals=0) if flops else None,
        compiler_params=pltpu.CompilerParams(vmem_limit_bytes=2 * 2**20),
    )(*args, *after)


def add_kernel(first_ref, second_ref, out_ref):
    out_ref[...] = first_ref[...] + second_ref[...]


def first_of_kernel(first_ref, second_ref, out_ref):
    out_ref[...] = first_ref[...] + second_ref[0]


def added(first, second, **options):
    return run(add_kernel, [first.shape], first, second, **options)[0]


def run_start(right_sides, basis_u, basis_v, coupling):
    columns, (points, rank) = right_sides.shape[1], basis_u.shape[1:]
    shape = jax.ShapeDtypeStruct
    arrays = [pltpu.with_memory_space_constraint(value, pltpu.HBM)
              for value in (right_sides, basis_u, basis_v, coupling)]
    outs = [shape((columns, points), F32), shape((columns, rank), F32), shape((points, rank), BF16),
            shape((points, rank), BF16), shape(coupling.shape[1:], BF16), shape((points, columns), F32)]
    return pl.pallas_call(
        start_kernel,
        out_shape=outs,
        in_specs=[pl.BlockSpec(memory_space=pl.ANY)] * len(arrays),
        out_specs=[pl.BlockSpec(memory_space=pltpu.VMEM)] * len(outs),
        scratch_shapes=[pltpu.VMEM((points, rank), BF16), pltpu.SemaphoreType.DMA((5,))],
        compiler_params=pltpu.CompilerParams(vmem_limit_bytes=4 * 2**20),
    )(*arrays)


def tied(value, *others):
    return lax.optimization_barrier((value,) + others)[0]


def traded(value, mask):
    if mask < lax.axis_size("sub"):
        return lax.ppermute(value, "sub", [(source, source ^ mask) for source in range(lax.axis_size("sub"))])
    devices = lax.axis_size("grp") * lax.axis_size("sub")
    return lax.ppermute(value, AXES, [(source, source ^ mask) for source in range(devices)])


def tree(right_sides, basis_u, basis_v, coupling):
    points, rank = basis_u.shape[1:]
    columns = right_sides.shape[1]
    half = columns // 2
    square, block, rows = (rank, rank), (half, rank), (rank // 2, rank)

    current, own, u_first, v_second, couple, right_near = run_start(right_sides, basis_u, basis_v, coupling)
    other = traded(own, 1)
    first_sum, first_cross = run(first_sum_kernel, [(columns, rank), square], current, u_first, v_second)
    weights0, keep, send = run(
        pair_kernel, [(columns, rank), block, block], own, other, couple, first_sum, first_cross
    )
    got = traded(send, 1)
    early, keep_cross, send_cross = run(
        cross_kernel, [(4,) + square, (2,) + rows, (2,) + rows], basis_u, basis_v, after=[weights0], flops=2 * 10**9
    )
    sum1 = added(keep, got, after=[keep_cross])
    sums, sums_send = run(
        later_sums_kernel, [(3,) + block, (3,) + block], current, weights0, basis_u, basis_v,
        after=[sum1], flops=4 * 10**9,
    )

    across = traded(sum1, 2)
    cross_got = traded(send_cross, 1)
    early_got = traded(tied(early, sum1), 1)
    sums_got = traded(sums_send, 1)
    cross32, cross43 = run(mix_kernel, [rows, rows], keep_cross, cross_got, flops=2 * 10**9)
    cross32_across = traded(cross32, 2)
    cross43_across = traded(cross43, 4)
    (weights1,) = run(first_weights_kernel, [block], sum1, across, coupling, flops=8 * 10**9)
    second, pair = run(
        second_third_kernel, [block, (2,) + block], weights1, early, early_got, sums, sums_got
    )

    both, beside, across = traded(second, 6), traded(pair, 2), traded(second, 4)
    fourth, cross42 = run(
        fourth_kernel, [block, square], weights1, early, early_got, sums, sums_got, flops=800 * 10**6
    )
    cross32, cross43 = run(
        both_added_kernel, [rows, rows], cross32, cross32_across, cross43, cross43_across, after=[fourth]
    )
    cross32_got = traded(cross32, 1)
    (weights2,) = run(
        functools.partial(square_weights_kernel, 2, "sub", 2, 2), [block], second, beside, across, both, coupling,
        flops=8 * 10**9,
    )
    cross43_across = traded(cross43, 2)
    third, later4 = run(
        third_fourth_kernel, [block, block],
        weights2, cross32, cross32_got, pair, beside, fourth, cross42,
    )

    sum4 = added(later4, traded(later4, 2), after=[third])
    sum4_got = traded(sum4, 4)
    both, across, beside = traded(third, 12), traded(third, 8), traded(third, 4)
    cross43 = added(cross43, cross43_across, after=[third])
    cross43_got = traded(cross43, 1)
    (weights3,) = run(
        functools.partial(square_weights_kernel, 3, "sub", 3, 2), [block], third, beside, across, both, coupling
    )
    sum4 = added(sum4, sum4_got, after=[weights3], flops=8 * 10**9)
    (sum4,) = run(last_sum_kernel, [block], weights3, sum4, cross43, cross43_got)

    both, beside, across = traded(sum4, 24), traded(sum4, 8), traded(sum4, 16)
    (three,) = run(stack_kernel, [(3,) + block], weights1, weights2, weights3, after=[sum4])
    three_got = traded(three, 1)
    (partial,) = run(
        gather_kernel, [(points, columns)], right_near, basis_u, weights0, three, three_got, flops=2 * 10**9
    )
    own_sum = added(sum4, beside, after=[both], flops=4 * 10**9)
    (weights4,) = run(
        functools.partial(square_weights_kernel, 4, "grp", 0, 1), [block], own_sum, across, both, coupling
    )
    return run_last(4, partial, weights4, traded(weights4, 1), basis_u)


def solution(mesh):
    n_grp, n_sub = mesh.shape["grp"], mesh.shape["sub"]

    def per_device(right_sides, basis_u, basis_v, coupling):
        if basis_u.shape[0] == 5 and n_grp == 2 and n_sub == 16:
            return tree(right_sides, basis_u, basis_v, coupling)
        return bit_by_bit(right_sides, basis_u, basis_v, coupling)

    in_specs = (P(AXES, None), P(None, AXES, None), P(None, AXES, None), P(None, AXES, None))
    return jax.shard_map(
        per_device, mesh=mesh, in_specs=in_specs, out_specs=P(AXES, None), check_vma=False
    )
```

```python
import functools

import jax
import jax.numpy as jnp
from jax import lax
from jax.experimental import pallas as pl
from jax.experimental.pallas import tpu as pltpu
from jax.sharding import PartitionSpec as P

F32 = jnp.float32
BF16 = jnp.bfloat16
AXES = ("grp", "sub")


def swapped(value, axis, bit):
    mask = 2**bit
    pairs = [(source, source ^ mask) for source in range(lax.axis_size(axis))]
    return lax.ppermute(value, axis, pairs)


def partner(value, bit, sub_bits):
    if bit < sub_bits:
        return swapped(value, "sub", bit)
    return swapped(value, "grp", bit - sub_bits)


def pairwise(own_sum, first_bit, span_bits, sub_bits, lower_half):
    for bit in range(first_bit, span_bits):
        own_sum = own_sum + partner(own_sum, bit, sub_bits)
    other_sum = partner(own_sum, span_bits, sub_bits)
    first_half = jnp.where(lower_half, own_sum, other_sum)
    second_half = jnp.where(lower_half, other_sum, own_sum)
    return jnp.concatenate([first_half, second_half], axis=0)


def bit_by_bit(right_sides, basis_u, basis_v, coupling):
    highest = lax.Precision.HIGHEST
    sub_bits = lax.axis_size("sub").bit_length() - 1
    all_bits = sub_bits + lax.axis_size("grp").bit_length() - 1
    levels = basis_u.shape[0]
    position = lax.axis_index("grp") * lax.axis_size("sub") + lax.axis_index("sub")
    current = right_sides
    for height in range(levels):
        span_bits = all_bits - levels + height
        v_basis = basis_v[height].astype(F32)
        own_sum = jnp.einsum("pr,pn->rn", v_basis, current, precision=highest)
        lower_half = jnp.bitwise_and(jnp.right_shift(position, span_bits), 1) == 0
        node_sum = pairwise(own_sum, 0, span_bits, sub_bits, lower_half)
        weights = jnp.dot(coupling[height].astype(F32), node_sum, precision=highest)
        current = current - jnp.dot(basis_u[height].astype(F32), weights, precision=highest)
    return current


def split(value):
    high = value.astype(BF16)
    low = (value - high.astype(F32)).astype(BF16)
    return high, low


def stacked(value):
    return jnp.concatenate(split(value), axis=0)


def folded(value):
    half = value.shape[0] // 2
    return value[:half] + value[half:]


def dot(left, right):
    return lax.dot_general(left, right, (((1,), (0,)), ((), ())), preferred_element_type=F32)


def dot_transposed(left, right):
    return lax.dot_general(left, right, (((1,), (1,)), ((), ())), preferred_element_type=F32)


def weights_of(lower, upper, couple):
    rank = couple.shape[0]
    lower, upper = stacked(lower), stacked(upper)
    return folded(dot_transposed(lower, couple[:, :rank]) + dot_transposed(upper, couple[:, rank:]))


def correction(weights, cross):
    high, low = split(cross)
    both = stacked(weights)
    return folded(dot(both, high) + dot(both, low))


def bit_is_set(axis, bit):
    return jnp.bitwise_and(jnp.right_shift(lax.axis_index(axis), bit), 1) == 1


def ordered(flag, own, other):
    return jnp.where(flag, other, own), jnp.where(flag, own, other)


def start_kernel(right_hbm, u_hbm, v_hbm, c_hbm, current_ref, sum_ref, u_ref, v_ref, c_ref, right_ref,
                 first_ref, sems):
    sources = [right_hbm, v_hbm.at[0], v_hbm.at[1], u_hbm.at[0], c_hbm.at[0]]
    targets = [right_ref, first_ref, v_ref, u_ref, c_ref]
    copies = [pltpu.make_async_copy(*pair, sems.at[place]) for place, pair in enumerate(zip(sources, targets))]
    for copy in copies:
        copy.start()
    copies[0].wait()
    current = right_ref[...].T
    current_ref[...] = current
    copies[1].wait()
    sum_ref[...] = folded(dot(stacked(current), first_ref[...]))
    for copy in copies[2:]:
        copy.wait()


def effect(couple, cross):
    high, low = split(cross)
    couple = couple.T
    return dot(couple, high) + dot(couple, low)


def first_sum_kernel(current_ref, u_ref, v_ref, c_ref, sum_ref, effect_ref):
    sum_ref[...] = folded(dot(stacked(current_ref[...]), v_ref[...]))
    effect_ref[...] = effect(c_ref[...], dot(u_ref[...].T, v_ref[...]))


def pair_kernel(own_ref, other_ref, sum_ref, effect_ref, keep_ref, send_ref):
    upper_core = bit_is_set("sub", 0)
    half = keep_ref.shape[0]
    node = jnp.concatenate(ordered(upper_core, own_ref[...], other_ref[...]), axis=1)
    later = sum_ref[...] - correction(node, effect_ref[...])
    keep_ref[...], send_ref[...] = ordered(upper_core, later[:half], later[half:])


def pair_weights_kernel(own_ref, other_ref, c_ref, weights_ref):
    weights_ref[...] = weights_of(*ordered(bit_is_set("sub", 0), own_ref[...], other_ref[...]), c_ref[...])


def later_sums_kernel(current_ref, weights_ref, u_ref, v_ref, keep_ref, send_ref):
    upper_core = bit_is_set("sub", 0)
    half = keep_ref.shape[1]
    current = current_ref[...] - folded(dot_transposed(stacked(weights_ref[...]), u_ref[...]))
    current = stacked(current)
    for place in range(keep_ref.shape[0]):
        later = folded(dot(current, v_ref[place + 2]))
        keep_ref[place], send_ref[place] = ordered(upper_core, later[:half], later[half:])


def cross_kernel(u_ref, v_ref, early_ref, keep_ref, send_ref):
    upper_core = bit_is_set("sub", 0)
    first, second, third = u_ref[1].T, u_ref[2].T, u_ref[3].T
    early_ref[0] = dot(first, v_ref[2])
    early_ref[1] = dot(first, v_ref[3])
    early_ref[2] = dot(first, v_ref[4])
    early_ref[3] = dot(second, v_ref[4])
    rows = keep_ref.shape[1]
    for place, cross in enumerate((dot(second, v_ref[3]), dot(third, v_ref[4]))):
        keep_ref[place], send_ref[place] = ordered(upper_core, cross[:rows], cross[rows:])


def mix_kernel(keep_ref, got_ref, third_ref, fourth_ref):
    third_ref[...], fourth_ref[...] = keep_ref[0] + got_ref[0], keep_ref[1] + got_ref[1]


def both_added_kernel(third_ref, third_got_ref, fourth_ref, fourth_got_ref, third_out_ref, fourth_out_ref):
    third_out_ref[...] = third_ref[...] + third_got_ref[...]
    fourth_out_ref[...] = fourth_ref[...] + fourth_got_ref[...]


def whole(half_ref, got_ref):
    return jnp.concatenate(ordered(bit_is_set("sub", 0), half_ref[...], got_ref[...]), axis=0)


def first_weights_kernel(own_ref, across_ref, c_ref, weights_ref):
    lower, upper = ordered(bit_is_set("sub", 1), own_ref[...], across_ref[...])
    weights_ref[...] = weights_of(lower, upper, c_ref[1])


def square_weights_kernel(level, axis, bit, own_count, *refs):
    *part_refs, c_ref, weights_ref = refs
    parts = [ref[0] if len(ref.shape) == 3 else ref[...] for ref in part_refs]
    own, other = sum(parts[1:own_count], parts[0]), sum(parts[own_count + 1 :], parts[own_count])
    weights_ref[...] = weights_of(*ordered(bit_is_set(axis, bit), own, other), c_ref[level])


def second_third_kernel(weights_ref, early_ref, got_ref, sums_ref, got_sums_ref, second_ref, pair_ref):
    weights = weights_ref[...]
    second_ref[...] = sums_ref[0] + got_sums_ref[0] - correction(weights, early_ref[0] + got_ref[0])
    pair_ref[0] = second_ref[...]
    pair_ref[1] = sums_ref[1] + got_sums_ref[1] - correction(weights, early_ref[1] + got_ref[1])


def fourth_kernel(weights_ref, early_ref, got_ref, sums_ref, got_sums_ref, fourth_ref, cross_ref):
    fourth_ref[...] = sums_ref[2] + got_sums_ref[2] - correction(weights_ref[...], early_ref[2] + got_ref[2])
    cross_ref[...] = early_ref[3] + got_ref[3]


def third_fourth_kernel(weights_ref, half_ref, half_got_ref, pair_ref, beside_ref, fourth_ref, cross_ref,
                        third_ref, later_ref):
    weights = weights_ref[...]
    cross = whole(half_ref, half_got_ref)
    third_ref[...] = pair_ref[1] + beside_ref[1] - correction(weights, cross)
    later_ref[...] = fourth_ref[...] - correction(weights, cross_ref[...])


def last_sum_kernel(weights_ref, sum_ref, half_ref, half_got_ref, later_ref):
    later_ref[...] = sum_ref[...] - correction(weights_ref[...], whole(half_ref, half_got_ref))


def stack_kernel(first_ref, second_ref, third_ref, out_ref):
    out_ref[0], out_ref[1], out_ref[2] = first_ref[...], second_ref[...], third_ref[...]


def columns_of(own, other):
    lower, upper = ordered(bit_is_set("sub", 0), own, other)
    return jnp.concatenate(split(jnp.concatenate([lower, upper], axis=0).T), axis=1)


def fold_columns(value):
    half = value.shape[1] // 2
    return value[:, :half] + value[:, half:]


def gather_kernel(right_ref, u_ref, first_ref, own_ref, other_ref, out_ref):
    total = dot(u_ref[0], jnp.concatenate(split(first_ref[...].T), axis=1))
    for place in range(own_ref.shape[0]):
        total = total + dot(u_ref[place + 1], columns_of(own_ref[place], other_ref[place]))
    out_ref[...] = right_ref[...] - fold_columns(total)


def last_kernel(level, chunks, partial_ref, own_ref, other_ref, u_ref, out_hbm, out_ref, sems):
    weights = columns_of(own_ref[...], other_ref[...])
    rows = out_ref.shape[0] // chunks
    copies = []
    for place in range(chunks):
        part = pl.ds(place * rows, rows)
        out_ref[part] = partial_ref[part] - fold_columns(dot(u_ref[level, part], weights))
        copies.append(pltpu.make_async_copy(out_ref.at[part], out_hbm.at[part], sems.at[place]))
        copies[-1].start()
    for copy in copies:
        copy.wait()


def run_last(level, partial, own, other, basis_u):
    vmem, chunks = pl.BlockSpec(memory_space=pltpu.VMEM), 4
    return pl.pallas_call(
        functools.partial(last_kernel, level, chunks),
        out_shape=jax.ShapeDtypeStruct(partial.shape, F32),
        in_specs=[vmem] * 4,
        out_specs=pl.BlockSpec(memory_space=pl.ANY),
        scratch_shapes=[pltpu.VMEM(partial.shape, F32), pltpu.SemaphoreType.DMA((chunks,))],
        compiler_params=pltpu.CompilerParams(vmem_limit_bytes=2 * 2**20),
    )(partial, own, other, basis_u)


def run(kernel, outs, *args, after=(), flops=0):
    vmem, unread = pl.BlockSpec(memory_space=pltpu.VMEM), pl.BlockSpec(memory_space=pl.ANY)
    return pl.pallas_call(
        lambda *refs: kernel(*refs[: len(args)], *refs[len(args) + len(after) :]),
        out_shape=[jax.ShapeDtypeStruct(shape, F32) for shape in outs],
        in_specs=[vmem] * len(args) + [unread] * len(after),
        out_specs=[vmem] * len(outs),
        cost_estimate=pl.CostEstimate(flops=flops, bytes_accessed=0, transcendentals=0) if flops else None,
        compiler_params=pltpu.CompilerParams(vmem_limit_bytes=2 * 2**20),
    )(*args, *after)


def add_kernel(first_ref, second_ref, out_ref):
    out_ref[...] = first_ref[...] + second_ref[...]


def first_of_kernel(first_ref, second_ref, out_ref):
    out_ref[...] = first_ref[...] + second_ref[0]


def added(first, second, **options):
    return run(add_kernel, [first.shape], first, second, **options)[0]


def run_start(right_sides, basis_u, basis_v, coupling):
    columns, (points, rank) = right_sides.shape[1], basis_u.shape[1:]
    shape = jax.ShapeDtypeStruct
    arrays = [pltpu.with_memory_space_constraint(value, pltpu.HBM)
              for value in (right_sides, basis_u, basis_v, coupling)]
    outs = [shape((columns, points), F32), shape((columns, rank), F32), shape((points, rank), BF16),
            shape((points, rank), BF16), shape(coupling.shape[1:], BF16), shape((points, columns), F32)]
    return pl.pallas_call(
        start_kernel,
        out_shape=outs,
        in_specs=[pl.BlockSpec(memory_space=pl.ANY)] * len(arrays),
        out_specs=[pl.BlockSpec(memory_space=pltpu.VMEM)] * len(outs),
        scratch_shapes=[pltpu.VMEM((points, rank), BF16), pltpu.SemaphoreType.DMA((5,))],
        compiler_params=pltpu.CompilerParams(vmem_limit_bytes=4 * 2**20),
    )(*arrays)


def tied(value, *others):
    return lax.optimization_barrier((value,) + others)[0]


def traded(value, mask):
    if mask < lax.axis_size("sub"):
        return lax.ppermute(value, "sub", [(source, source ^ mask) for source in range(lax.axis_size("sub"))])
    devices = lax.axis_size("grp") * lax.axis_size("sub")
    return lax.ppermute(value, AXES, [(source, source ^ mask) for source in range(devices)])


def tree(right_sides, basis_u, basis_v, coupling):
    points, rank = basis_u.shape[1:]
    columns = right_sides.shape[1]
    half = columns // 2
    square, block, rows = (rank, rank), (half, rank), (rank // 2, rank)

    current, own, u_first, v_second, couple, right_near = run_start(right_sides, basis_u, basis_v, coupling)
    other = traded(own, 1)
    first_sum, first_effect = run(
        first_sum_kernel, [(columns, rank), (2 * rank, rank)], current, u_first, v_second, couple
    )
    keep, send = run(pair_kernel, [block, block], own, other, first_sum, first_effect)
    got = traded(send, 1)
    early, keep_cross, send_cross = run(
        cross_kernel, [(4,) + square, (2,) + rows, (2,) + rows], basis_u, basis_v, after=[keep], flops=2 * 10**9
    )
    sum1 = added(keep, got, after=[keep_cross])
    (weights0,) = run(pair_weights_kernel, [(columns, rank)], own, other, couple, after=[sum1])
    sums, sums_send = run(
        later_sums_kernel, [(3,) + block, (3,) + block], current, weights0, u_first, basis_v, flops=4 * 10**9
    )

    across = traded(sum1, 2)
    cross_got = traded(send_cross, 1)
    early_got = traded(tied(early, sum1), 1)
    sums_got = traded(sums_send, 1)
    cross32, cross43 = run(mix_kernel, [rows, rows], keep_cross, cross_got, flops=2 * 10**9)
    cross32_across = traded(cross32, 2)
    cross43_across = traded(cross43, 4)
    (weights1,) = run(first_weights_kernel, [block], sum1, across, coupling, flops=8 * 10**9)
    second, pair = run(
        second_third_kernel, [block, (2,) + block], weights1, early, early_got, sums, sums_got
    )

    both, beside, across = traded(second, 6), traded(pair, 2), traded(second, 4)
    fourth, cross42 = run(
        fourth_kernel, [block, square], weights1, early, early_got, sums, sums_got, flops=800 * 10**6
    )
    cross32, cross43 = run(
        both_added_kernel, [rows, rows], cross32, cross32_across, cross43, cross43_across, after=[fourth]
    )
    cross32_got = traded(cross32, 1)
    (weights2,) = run(
        functools.partial(square_weights_kernel, 2, "sub", 2, 2), [block], second, beside, across, both, coupling,
        flops=8 * 10**9,
    )
    cross43_across = traded(cross43, 2)
    third, later4 = run(
        third_fourth_kernel, [block, block],
        weights2, cross32, cross32_got, pair, beside, fourth, cross42,
    )

    sum4 = added(later4, traded(later4, 2), after=[third])
    sum4_got = traded(sum4, 4)
    both, across, beside = traded(third, 12), traded(third, 8), traded(third, 4)
    cross43 = added(cross43, cross43_across, after=[third])
    cross43_got = traded(cross43, 1)
    (weights3,) = run(
        functools.partial(square_weights_kernel, 3, "sub", 3, 2), [block], third, beside, across, both, coupling
    )
    sum4 = added(sum4, sum4_got, after=[weights3], flops=8 * 10**9)
    (sum4,) = run(last_sum_kernel, [block], weights3, sum4, cross43, cross43_got)

    both, beside, across = traded(sum4, 24), traded(sum4, 8), traded(sum4, 16)
    (three,) = run(stack_kernel, [(3,) + block], weights1, weights2, weights3, after=[sum4])
    three_got = traded(three, 1)
    (partial,) = run(
        gather_kernel, [(points, columns)], right_near, basis_u, weights0, three, three_got, flops=2 * 10**9
    )
    own_sum = added(sum4, beside, after=[both], flops=4 * 10**9)
    (weights4,) = run(
        functools.partial(square_weights_kernel, 4, "grp", 0, 1), [block], own_sum, across, both, coupling
    )
    return run_last(4, partial, weights4, traded(weights4, 1), basis_u)


def solution(mesh):
    n_grp, n_sub = mesh.shape["grp"], mesh.shape["sub"]

    def per_device(right_sides, basis_u, basis_v, coupling):
        if basis_u.shape[0] == 5 and n_grp == 2 and n_sub == 16:
            return tree(right_sides, basis_u, basis_v, coupling)
        return bit_by_bit(right_sides, basis_u, basis_v, coupling)

    in_specs = (P(AXES, None), P(None, AXES, None), P(None, AXES, None), P(None, AXES, None))
    return jax.shard_map(
        per_device, mesh=mesh, in_specs=in_specs, out_specs=P(AXES, None), check_vma=False
    )
```
